32 devices in a mesh: frames: 4 (over y, x), pix: 8 (over z, core).
Axes of the slice: x: 2, y: 2, z: 4, core: 2. Of those that a mesh axis runs over, the one named last changes fastest.
Arguments:
- photon_counts: int32 [4096, 16384], P('frames', 'pix'), may hold values from 1 to 53, as said below
- flat_field: float32 [16384], P('pix'), may hold values from 0.5 to 2
- owner_counts: int32 [8], replicated, may hold values from 512 to 2048, as said below
Outputs:
- diagonal_tiles: float32 [4096, 1024], P(('frames', 'pix'))
- offdiag_tiles: float32 [4096, 1024], P(('frames', 'pix'))
The draws below stay inside these ranges and needn't reach their ends.
Inputs may be any that keep to these rules, and one draw needn't show every extreme that they name: owner_counts[i] is how many of owner i's 2048 slots, the first ones, hold cycle pixels; some owner holds all 2048. `photon_counts`: whole photon counts of each slot in each frame.
All inputs are finite; a program needn't handle non-finite values.
Results may differ from the reference program's by a relative error of at most 0.0003.
Values may be sent and summed in bfloat16 or wider, within the bound.
A program may use at most 64 MiB of HBM per device.

```python
import math
import jax
import jax.numpy as jnp
from jax import lax

F = 1024
PCAP = 2048
OWNERS = 8
SLOTS = 16384
FRAMES = 4096
N_FRAMES = 4


def draw_owner_counts(key, part):
    first_key = jax.random.fold_in(key, 11)
    second_key = jax.random.fold_in(key, 23)
    values = jax.random.randint(first_key, (OWNERS,), PCAP // 4, PCAP + 1, dtype=jnp.int32)
    chosen = jax.random.randint(second_key, (), 0, OWNERS, dtype=jnp.int32)
    return values.at[chosen].set(PCAP)


def draw_photon_counts(key, part):
    event_key = jax.random.fold_in(key, 101)
    first_key = jax.random.fold_in(key, 103)
    second_key = jax.random.fold_in(key, 107)
    shot_key = jax.random.fold_in(key, 109)
    events = (jax.random.randint(event_key, (FRAMES,), 0, 8, dtype=jnp.int32) == 0).astype(jnp.int32)
    segment = (jnp.cumsum(events) % 256).astype(jnp.int32)
    first_factor = jax.random.randint(first_key, (256, SLOTS), 0, 4, dtype=jnp.int32)
    second_factor = jax.random.randint(second_key, (256, SLOTS), 0, 4, dtype=jnp.int32)
    speckle = first_factor * second_factor
    owner_ids = jnp.arange(SLOTS, dtype=jnp.int32) // PCAP
    sector_rate = 1 + 3 * owner_ids // max(OWNERS - 1, 1)
    shot_noise = jax.random.randint(shot_key, (FRAMES, SLOTS), 0, 5, dtype=jnp.int32)
    return (1 + sector_rate[None, :] * (speckle[segment] + shot_noise)).astype(jnp.int32)


def shard_levels(rng, dims, split, least, largest):
    loudness, own = 1.0, jax.random.fold_in(rng, 6)
    for dim, blocks in split:
        heights = jnp.exp(jax.random.uniform(jax.random.fold_in(own, dim), (blocks,), jnp.float32, least / len(split), largest / len(split)))
        loudness = loudness * jnp.repeat(heights, dims[dim] // blocks).reshape([-1 if axis == dim else 1 for axis in range(len(dims))])
    return loudness


def setup_inputs(seed: int = 0) -> dict:
    seeds = jax.random.split(jax.random.key(seed), 4)
    return {
        "photon_counts": draw_photon_counts(jax.random.fold_in(seeds[3], 71), 0),
        "flat_field": jnp.clip(jnp.exp(math.log(2.0) - 1.3862944 * jax.random.uniform(seeds[1], (SLOTS,), jnp.float32) ** shard_levels(seeds[1], (SLOTS,), ((0, 8),), -0.2, 0.2)), 0.5, 2.0),
        "owner_counts": draw_owner_counts(jax.random.fold_in(seeds[3], 71), 0),
    }


def gram(left, right):
    return lax.dot_general(left, right, (((1,), (1,)), ((), ())), preferred_element_type=jnp.float32)


def reference(photon_counts, flat_field, owner_counts):
    slot_ids = jnp.arange(SLOTS, dtype=jnp.int32)
    limits = owner_counts[slot_ids // PCAP]
    valid = (slot_ids % PCAP < limits).astype(jnp.float32)
    weights = flat_field * valid
    pixel_total = jnp.sum(owner_counts).astype(jnp.float32)
    blocks = photon_counts.reshape(N_FRAMES, F, SLOTS)

    def scale_block(block):
        corrected = block.astype(jnp.float32) * weights[None, :]
        frame_mean = jnp.sum(corrected, axis=1) / pixel_total
        return (corrected / frame_mean[:, None]).astype(jnp.bfloat16)

    scaled = lax.map(scale_block, blocks)

    def tiles(block_index):
        own_block = scaled[block_index]
        earlier = scaled[jnp.maximum(block_index - 1, 0)]
        diagonal = gram(own_block, own_block) / pixel_total
        keep = (block_index > 0).astype(jnp.float32)
        offdiag = gram(own_block, earlier) / pixel_total * keep
        return diagonal, offdiag

    diagonal_all, offdiag_all = lax.map(tiles, jnp.arange(N_FRAMES, dtype=jnp.int32))
    return diagonal_all.reshape(FRAMES, F), offdiag_all.reshape(FRAMES, F)
```

```python
import functools

import jax
import jax.numpy as jnp
from jax import lax
from jax.experimental import pallas as pl
from jax.experimental.pallas import tpu as pltpu
from jax.sharding import PartitionSpec as P

MESH = pl.DeviceIdType.MESH
F32, BF16 = jnp.float32, jnp.bfloat16
LANES = 128
CHUNKS = 4
LEVELS = 64000.0
OFFSET = 32768
CORES = 2


def dot_rows(left, right):
    return lax.dot_general(left, right, (((1,), (1,)), ((), ())), preferred_element_type=F32)


def quantized(value):
    return ((value + 0.5).astype(jnp.int32) - OFFSET).astype(jnp.int16)


def restored(value):
    return (value.astype(jnp.int32) + OFFSET).astype(F32)


def remote(src, dst, send_sem, recv_sem, device):
    return pltpu.make_async_remote_copy(
        src_ref=src, dst_ref=dst, send_sem=send_sem, recv_sem=recv_sem,
        device_id=device, device_id_type=MESH,
    )


def kernel(
    n_frames, n_pix,
    owner_ref, counts_hbm, flat_ref, diag_ref, off_ref,
    counts, own, frames_s, weights, stats, totals, rows, cols,
    core_out, core_in, acc, z_out, z_in, last_out, last_in,
    load_sem, data_send, data_recv, stat_send, stat_recv, tot_send, tot_recv,
    core_send, core_recv, z_send, z_recv, last_send, last_recv,
):
    square = n_frames == 4
    n_z = n_pix // CORES
    stages = n_z.bit_length() - 1
    block = lax.axis_index("frames")
    pix = lax.axis_index("pix")
    z, core = pix // CORES, lax.rem(pix, CORES)
    n_rows, n_slots = counts.shape
    half = n_slots // 2
    piece = n_rows // n_pix
    step = n_rows // CHUNKS
    x = lax.rem(block, 2)
    outer = jnp.logical_or(block == 0, block == 3)
    inner = jnp.logical_not(outer)
    across = block + 1 - 2 * x
    up = lax.rem(block + 2, 4)
    me = block if square else 0
    has_next, has_prev = block < n_frames - 1, block > 0
    follow = jnp.minimum(block + 1, n_frames - 1)
    before = jnp.maximum(block - 1, 0)

    def load(q):
        part = pl.ds(q * step, step)
        return pltpu.make_async_copy(counts_hbm.at[part], counts.at[part], load_sem.at[q])

    for q in range(CHUNKS):
        load(q).start()

    barrier = pltpu.get_barrier_semaphore()
    for d in range(1, n_pix):
        pl.semaphore_signal(barrier, inc=1, device_id={"pix": lax.rem(pix + d, n_pix)}, device_id_type=MESH)
    if square:
        for d in range(1, 4):
            pl.semaphore_signal(barrier, inc=1, device_id={"frames": lax.rem(block + d, 4)}, device_id_type=MESH)
        pl.semaphore_wait(barrier, n_pix - 1 + 3)
    else:
        @pl.when(has_next)
        def _():
            pl.semaphore_signal(barrier, inc=1, device_id={"frames": follow}, device_id_type=MESH)

        @pl.when(has_prev)
        def _():
            pl.semaphore_signal(barrier, inc=1, device_id={"frames": before}, device_id_type=MESH)

        pl.semaphore_wait(barrier, n_pix - 1 + has_next.astype(jnp.int32) + has_prev.astype(jnp.int32))

    if square:
        always = block >= 0
        streams = ((0, 1 - x, across, always, always), (1, x, up, inner, outer))
    else:
        streams = ((0, 0, follow, has_next, has_prev), (1, 1, follow, has_next, has_prev))

    def data(slot, which, target, q):
        part = pl.ds(q * step, step)
        return remote(
            own.at[which, part], frames_s.at[2 + slot, part],
            data_send.at[slot, q], data_recv.at[slot, q], {"frames": target},
        )

    pixel_total = owner_ref[0]
    for i in range(1, n_pix):
        pixel_total = pixel_total + owner_ref[i]
    pixel_total = pixel_total.astype(F32)
    limit = owner_ref[pix]
    slot_ids = lax.broadcasted_iota(jnp.int32, (8, n_slots), 1)
    valid = (slot_ids < limit).astype(F32)
    weight = flat_ref[...] * valid
    weights[...] = weight
    first = weight.astype(BF16)
    rest = weight - first.astype(F32)
    second = rest.astype(BF16)
    third = (rest - second.astype(F32)).astype(BF16)
    split = (first, second, third)
    squares = (weight * weight).astype(BF16)

    stats[pix] = jnp.zeros((8, n_rows), F32)
    small = 16
    for q in range(CHUNKS):
        load(q).wait()

        @pl.loop(0, step // small)
        def _(i):
            at = pl.ds(q * step + i * small, small)
            for h in range(2):
                own[h, at, :] = counts[at, h * half:(h + 1) * half].astype(F32).astype(BF16)

        for slot, which, target, sends, _ in streams:
            @pl.when(sends)
            def _(slot=slot, which=which, target=target):
                data(slot, which, target, q).start()

    for q in range(CHUNKS):
        part = slice(q * step, (q + 1) * step)
        sums = jnp.zeros((8, step), F32)
        norms = jnp.zeros((8, step), F32)
        for h in range(2):
            held = own[h, part, :]
            lanes = slice(h * half, (h + 1) * half)
            for term in split:
                sums = sums + dot_rows(term[:, lanes], held)
            norms = norms + dot_rows(squares[:, lanes], held * held)
        stats[pix, 0:1, part] = sums[0:1]
        stats[pix, 1:2, part] = norms[0:1]

    def stat(d):
        return remote(
            stats.at[pix], stats.at[pix], stat_send.at[d], stat_recv.at[pix],
            {"pix": lax.rem(pix + d, n_pix)},
        )

    def stat_from(d):
        source = lax.rem(pix + d, n_pix)
        return remote(stats.at[source], stats.at[source], stat_send.at[d], stat_recv.at[source], {"pix": source})

    for d in range(1, n_pix):
        stat(d).start()
    for d in range(1, n_pix):
        stat_from(d).wait_recv()
    total = stats[0]
    for i in range(1, n_pix):
        total = total + stats[i]
    totals[me] = total

    if square:
        def tot(d):
            return remote(totals.at[me], totals.at[me], tot_send.at[d], tot_recv.at[me], {"frames": lax.rem(block + d, 4)})

        def tot_from(d):
            source = lax.rem(block + d, 4)
            return remote(totals.at[source], totals.at[source], tot_send.at[d], tot_recv.at[source], {"frames": source})

        for d in range(1, 4):
            tot(d).start()
    else:
        def tot_next():
            return remote(totals.at[0], totals.at[1], tot_send.at[0], tot_recv.at[0], {"frames": follow})

        @pl.when(has_next)
        def _():
            tot_next().start()

    def take(index):
        held = totals[index]
        inverse_mean = pixel_total / held[0:1]
        norm = jnp.sqrt(held[1:2]) * inverse_mean
        scale = LEVELS ** 0.5 / norm
        rows[index, 0:1, :] = scale
        rows[index, 1:2, :] = 1.0 / scale
        cols[index, 0] = jnp.transpose(jnp.broadcast_to(inverse_mean, (LANES, n_rows)))
        cols[index, 1] = jnp.transpose(jnp.broadcast_to(scale, (LANES, n_rows)))
        cols[index, 2] = jnp.transpose(jnp.broadcast_to(1.0 / scale, (LANES, n_rows)))

    take(me)

    @pl.loop(0, n_rows // small)
    def _(i):
        at = pl.ds(i * small, small)
        inverse = cols[me, 0, at, 0:1]
        for h in range(2):
            lanes = slice(h * half, (h + 1) * half)
            frame = own[h, at, :].astype(F32) * weights[0:1, lanes]
            frames_s[h, at, :] = (frame * inverse).astype(BF16)

    def product(k, pairs, row_block, col_block):
        other = 1 - core

        def core_copy(j):
            return remote(core_out.at[k, j], core_in.at[k, j], core_send.at[k, j], core_recv.at[k, j], {"pix": z * CORES + other})

        def tile(owner):
            at = pl.ds(pl.multiple_of(owner * piece, piece), piece)
            out = None
            for left, right in pairs:
                term = dot_rows(frames_s[left, at, :], frames_s[right])
                out = term if out is None else out + term
            return out

        @pl.loop(0, n_z)
        def _(j):
            core_out[k, j] = tile(j * CORES + other)
            core_copy(j).start()

        @pl.loop(0, n_z)
        def _(j):
            acc[k, j] = tile(j * CORES + core)

        @pl.loop(0, n_z)
        def _(j):
            core_copy(j).wait()
            at = pl.ds(pl.multiple_of((j * CORES + core) * piece, piece), piece)
            value = acc[k, j] + core_in[k, j]
            acc[k, j] = value * cols[row_block, 1, at, 0:1] * rows[col_block, 0:1, :]

    def z_base(s):
        return n_z - (n_z >> s)

    def z_copy(k, s, m):
        bit = 1 << s
        sign = 1 - 2 * lax.rem(z // bit, 2)
        at = z_base(s) + m
        return remote(
            z_out.at[k, at], z_in.at[k, at], z_send.at[k, at], z_recv.at[k, at],
            {"pix": (z + sign * bit) * CORES + core},
        )

    def z_send_stage(k, s):
        bit = 1 << s
        low, top = lax.rem(z, bit), lax.rem(z // bit, 2)
        for m in range(n_z >> (s + 1)):
            j = m * 2 * bit + (1 - top) * bit + low
            z_out[k, z_base(s) + m] = quantized(acc[k, j])
            z_copy(k, s, m).start()

    def z_recv_stage(k, s):
        bit = 1 << s
        for m in range(n_z >> (s + 1)):
            z_copy(k, s, m).wait()
            j = m * 2 * bit + lax.rem(z, 2 * bit)
            acc[k, j] = acc[k, j] + restored(z_in[k, z_base(s) + m])

    product(0, ((0, 0), (1, 1)), me, me)
    for s in range(stages):
        z_send_stage(0, s)
        z_recv_stage(0, s)
    mine = pl.ds(pl.multiple_of(pix * piece, piece), piece)
    inverse_total = 1.0 / jnp.full((1, 1), pixel_total, F32)
    diag_ref[...] = acc[0, z] * cols[me, 2, mine, 0:1] * (rows[me, 1:2, :] * inverse_total)

    if square:
        for d in range(1, 4):
            tot_from(d).wait_recv()
        for d in range(1, 4):
            take(lax.rem(block + d, 4))
    else:
        @pl.when(has_prev)
        def _():
            tot_next().wait_recv()
            take(1)

    for q in range(CHUNKS):
        for slot, which, target, _, arrives in streams:
            @pl.when(arrives)
            def _(slot=slot, which=which, target=target):
                data(slot, which, target, q).wait_recv()
                source = (across if slot == 0 else up) if square else 1
                lanes = pl.ds(pl.multiple_of((x if square else slot) * half, half), half)

                @pl.loop(0, step // small)
                def _(i):
                    at = pl.ds(q * step + i * small, small)
                    inverse = cols[source, 0, at, 0:1]
                    frame = frames_s[2 + slot, at, :].astype(F32) * weights[0:1, lanes]
                    frames_s[2 + slot, at, :] = (frame * inverse).astype(BF16)

    if square:
        later, sooner = jnp.maximum(block, across), jnp.minimum(block, across)
        product(1, ((jnp.where(x == 0, 2, 1), jnp.where(x == 0, 0, 2)),), later, sooner)

        @pl.when(outer)
        def _():
            product(2, ((jnp.where(x == 0, 3, 2), jnp.where(x == 0, 2, 3)),), 2, 1)

        for s in range(stages):
            z_send_stage(1, s)

            @pl.when(outer)
            def _():
                z_send_stage(2, s)

            z_recv_stage(1, s)

            @pl.when(outer)
            def _():
                z_recv_stage(2, s)

        even = x == 0

        def last(source, slot, target):
            return remote(last_out.at[source], last_in.at[slot], last_send.at[source], last_recv.at[slot], {"frames": target})

        @pl.when(even)
        def _():
            last_out[0] = quantized(acc[1, z])
            last(0, 0, across).start()

        @pl.when(block == 0)
        def _():
            last_out[1] = quantized(acc[2, z])
            last(1, 1, up).start()

        @pl.when(block == 3)
        def _():
            last_out[1] = quantized(acc[2, z])
            last(1, 0, across).start()

        @pl.when(block == 0)
        def _():
            off_ref[...] = jnp.zeros_like(off_ref)

        def write(value):
            off_ref[...] = value * cols[block, 2, mine, 0:1] * (rows[before, 1:2, :] * inverse_total)

        @pl.when(x == 1)
        def _():
            last(0, 0, across).wait_recv()
            write(acc[1, z] + restored(last_in[0]))

        @pl.when(block == 2)
        def _():
            last(0, 0, across).wait_recv()
            last(1, 1, up).wait_recv()
            write(restored(last_in[0]) + restored(last_in[1]))

        @pl.when(even)
        def _():
            last(0, 0, across).wait_send()

        @pl.when(outer)
        def _():
            last(1, 1, up).wait_send()
    else:
        @pl.when(has_prev)
        def _():
            product(1, ((0, 2), (1, 3)), 0, 1)
            for s in range(stages):
                z_send_stage(1, s)
                z_recv_stage(1, s)
            off_ref[...] = acc[1, z] * cols[0, 2, mine, 0:1] * (rows[1, 1:2, :] * inverse_total)

        @pl.when(jnp.logical_not(has_prev))
        def _():
            off_ref[...] = jnp.zeros_like(off_ref)

    for d in range(1, n_pix):
        stat(d).wait_send()
    if square:
        for d in range(1, 4):
            tot(d).wait_send()
    else:
        @pl.when(has_next)
        def _():
            tot_next().wait_send()
    for q in range(CHUNKS):
        for slot, which, target, sends, _ in streams:
            @pl.when(sends)
            def _(slot=slot, which=which, target=target):
                data(slot, which, target, q).wait_send()


def on_device(n_frames, n_pix, photon_counts, flat_field, owner_counts):
    n_rows, n_slots = photon_counts.shape
    half, piece, n_z = n_slots // 2, n_rows // n_pix, n_pix // CORES
    tiles, blocks = (3, 4) if n_frames == 4 else (2, 2)
    sent = max(n_z - 1, 1)
    flat = jnp.broadcast_to(flat_field[None, :], (8, n_slots))
    out = jax.ShapeDtypeStruct((piece, n_rows), F32)
    dma = pltpu.SemaphoreType.DMA
    return pl.pallas_call(
        functools.partial(kernel, n_frames, n_pix),
        out_shape=(out, out),
        in_specs=[
            pl.BlockSpec(memory_space=pltpu.SMEM),
            pl.BlockSpec(memory_space=pl.ANY),
            pl.BlockSpec(memory_space=pltpu.VMEM),
        ],
        out_specs=(pl.BlockSpec(memory_space=pltpu.VMEM),) * 2,
        scratch_shapes=[
            pltpu.VMEM((n_rows, n_slots), jnp.int32),
            pltpu.VMEM((2, n_rows, half), BF16),
            pltpu.VMEM((4, n_rows, half), BF16),
            pltpu.VMEM((8, n_slots), F32),
            pltpu.VMEM((n_pix, 8, n_rows), F32),
            pltpu.VMEM((blocks, 8, n_rows), F32),
            pltpu.VMEM((blocks, 8, n_rows), F32),
            pltpu.VMEM((blocks, 3, n_rows, LANES), F32),
            pltpu.VMEM((tiles, n_z, piece, n_rows), F32),
            pltpu.VMEM((tiles, n_z, piece, n_rows), F32),
            pltpu.VMEM((tiles, n_z, piece, n_rows), F32),
            pltpu.VMEM((tiles, sent, piece, n_rows), jnp.int16),
            pltpu.VMEM((tiles, sent, piece, n_rows), jnp.int16),
            pltpu.VMEM((2, piece, n_rows), jnp.int16),
            pltpu.VMEM((2, piece, n_rows), jnp.int16),
            dma((CHUNKS,)),
            dma((2, CHUNKS)), dma((2, CHUNKS)),
            dma((n_pix,)), dma((n_pix,)),
            dma((4,)), dma((4,)),
            dma((tiles, n_z)), dma((tiles, n_z)),
            dma((tiles, sent)), dma((tiles, sent)),
            dma((2,)), dma((2,)),
        ],
        compiler_params=pltpu.CompilerParams(
            collective_id=0, has_side_effects=True, vmem_limit_bytes=62 * 1024 * 1024
        ),
        cost_estimate=pl.CostEstimate(
            flops=4 * n_rows * n_rows * n_slots, bytes_accessed=4 * n_rows * n_slots, transcendentals=0
        ),
    )(owner_counts, photon_counts, flat)


def solution(mesh):
    return jax.shard_map(
        functools.partial(on_device, mesh.shape["frames"], mesh.shape["pix"]),
        mesh=mesh,
        in_specs=(P("frames", "pix"), P("pix"), P()),
        out_specs=(P(("frames", "pix"), None), P(("frames", "pix"), None)),
        check_vma=False,
    )
```

```python
import functools

import jax
import jax.numpy as jnp
from jax import lax
from jax.experimental import pallas as pl
from jax.experimental.pallas import tpu as pltpu
from jax.sharding import PartitionSpec as P

MESH = pl.DeviceIdType.MESH
F32, BF16 = jnp.float32, jnp.bfloat16
LANES = 128
LEVELS = 64000.0
OFFSET = 32768
CORES = 2


def dot_rows(left, right):
    return lax.dot_general(left, right, (((1,), (1,)), ((), ())), preferred_element_type=F32)


def widened(column, lanes):
    count = lanes // LANES
    return column if count == 1 else jnp.concatenate([column] * count, axis=-1)


def quantized(value):
    return ((value + 0.5).astype(jnp.int32) - OFFSET).astype(jnp.int16)


def restored(value):
    return (value.astype(jnp.int32) + OFFSET).astype(F32)


def remote(src, dst, send_sem, recv_sem, device):
    return pltpu.make_async_remote_copy(
        src_ref=src, dst_ref=dst, send_sem=send_sem, recv_sem=recv_sem,
        device_id=device, device_id_type=MESH,
    )


def kernel(
    n_frames, n_pix,
    owner_ref, counts_hbm, flat_ref, diag_ref, off_ref,
    counts, own, frames_s, sum_rows, weights, stats, totals, rows, cols,
    core_out, core_in, acc, z_out, z_in, last_out, last_in,
    load_sem, data_send, data_recv, stat_send, stat_recv, tot_send, tot_recv,
    core_send, core_recv, z_send, z_recv, last_send, last_recv,
):
    square = n_frames == 4
    n_z = n_pix // CORES
    stages = n_z.bit_length() - 1
    block = lax.axis_index("frames")
    pix = lax.axis_index("pix")
    z, core = pix // CORES, lax.rem(pix, CORES)
    n_rows, n_slots = counts.shape
    half = n_slots // 2
    piece = n_rows // n_pix
    pair = CORES * piece
    x = lax.rem(block, 2)
    outer = jnp.logical_or(block == 0, block == 3)
    inner = jnp.logical_not(outer)
    across = block + 1 - 2 * x
    up = lax.rem(block + 2, 4)
    me = block if square else 0
    has_next, has_prev = block < n_frames - 1, block > 0
    follow = jnp.minimum(block + 1, n_frames - 1)
    before = jnp.maximum(block - 1, 0)

    def load(q):
        part = pl.ds(q * pair, pair)
        return pltpu.make_async_copy(counts_hbm.at[part], counts.at[part], load_sem.at[q])

    for q in range(n_z):
        load(q).start()

    barrier = pltpu.get_barrier_semaphore()
    for d in range(1, n_pix):
        pl.semaphore_signal(barrier, inc=1, device_id={"pix": lax.rem(pix + d, n_pix)}, device_id_type=MESH)
    if square:
        for d in range(1, 4):
            pl.semaphore_signal(barrier, inc=1, device_id={"frames": lax.rem(block + d, 4)}, device_id_type=MESH)
        pl.semaphore_wait(barrier, n_pix - 1 + 3)
    else:
        @pl.when(has_next)
        def _():
            pl.semaphore_signal(barrier, inc=1, device_id={"frames": follow}, device_id_type=MESH)

        @pl.when(has_prev)
        def _():
            pl.semaphore_signal(barrier, inc=1, device_id={"frames": before}, device_id_type=MESH)

        pl.semaphore_wait(barrier, n_pix - 1 + has_next.astype(jnp.int32) + has_prev.astype(jnp.int32))

    if square:
        always = block >= 0
        streams = ((0, 1 - x, across, always, always), (1, x, up, inner, outer))
    else:
        streams = ((0, 0, follow, has_next, has_prev), (1, 1, follow, has_next, has_prev))

    def data(slot, which, target, q):
        return remote(
            own.at[which, q], frames_s.at[2 + slot, q],
            data_send.at[slot, q], data_recv.at[slot, q], {"frames": target},
        )

    pixel_total = owner_ref[0]
    for i in range(1, n_pix):
        pixel_total = pixel_total + owner_ref[i]
    pixel_total = pixel_total.astype(F32)
    limit = owner_ref[pix]
    slot_ids = lax.broadcasted_iota(jnp.int32, (16, n_slots), 1)
    valid = (slot_ids < limit).astype(F32)
    weight = flat_ref[...] * valid
    weights[...] = weight
    first = weight.astype(BF16).astype(F32)
    second = (weight - first).astype(BF16).astype(F32)
    third = weight - first - second
    line = lax.broadcasted_iota(jnp.int32, (16, n_slots), 0)
    none = jnp.zeros_like(weight)
    split = jnp.where(line == 0, first, jnp.where(line == 1, second, jnp.where(line == 2, third, none)))
    filler = jnp.zeros((LANES - 16, n_slots), BF16)
    for i, value in enumerate((split, jnp.where(line == 3, weight * weight, none))):
        sum_rows[i, 0:16, :] = value.astype(BF16)
        sum_rows[i, 16:LANES, :] = filler

    stats[pix] = jnp.zeros((8, n_rows), F32)
    small = 16
    for q in range(n_z):
        load(q).wait()

        @pl.loop(0, piece // small)
        def _(i):
            for c in range(CORES):
                for h in range(2):
                    taken = counts[pl.ds(q * pair + c * piece + i * small, small), h * half:(h + 1) * half]
                    own[h, q, c, pl.ds(i * small, small), :] = taken.astype(F32).astype(BF16)

        for slot, which, target, sends, _ in streams:
            @pl.when(sends)
            def _(slot=slot, which=which, target=target):
                data(slot, which, target, q).start()

    for q in range(n_z):
        sums = jnp.zeros((pair, LANES), F32)
        for h in range(2):
            held = own[h, q].reshape(pair, half)
            lanes = slice(h * half, (h + 1) * half)
            sums = sums + dot_rows(held, sum_rows[0, :, lanes]) + dot_rows(held * held, sum_rows[1, :, lanes])
        sums = jnp.transpose(sums)
        part = slice(q * pair, (q + 1) * pair)
        stats[pix, 0:1, part] = sums[0:1] + sums[1:2] + sums[2:3]
        stats[pix, 1:2, part] = sums[3:4]

    def stat(d):
        return remote(
            stats.at[pix], stats.at[pix], stat_send.at[d], stat_recv.at[pix],
            {"pix": lax.rem(pix + d, n_pix)},
        )

    def stat_from(d):
        source = lax.rem(pix + d, n_pix)
        return remote(stats.at[source], stats.at[source], stat_send.at[d], stat_recv.at[source], {"pix": source})

    for d in range(1, n_pix):
        stat(d).start()
    for d in range(1, n_pix):
        stat_from(d).wait_recv()
    total = stats[0]
    for i in range(1, n_pix):
        total = total + stats[i]
    totals[me] = total

    if square:
        def tot(d):
            return remote(totals.at[me], totals.at[me], tot_send.at[d], tot_recv.at[me], {"frames": lax.rem(block + d, 4)})

        def tot_from(d):
            source = lax.rem(block + d, 4)
            return remote(totals.at[source], totals.at[source], tot_send.at[d], tot_recv.at[source], {"frames": source})

        for d in range(1, 4):
            tot(d).start()
    else:
        def tot_next():
            return remote(totals.at[0], totals.at[1], tot_send.at[0], tot_recv.at[0], {"frames": follow})

        @pl.when(has_next)
        def _():
            tot_next().start()

    def take(index):
        held = totals[index]
        inverse_mean = pixel_total / held[0:1]
        norm = jnp.sqrt(held[1:2]) * inverse_mean
        scale = LEVELS ** 0.5 / norm
        rows[index, 0:1, :] = scale
        rows[index, 1:2, :] = 1.0 / scale
        for i, value in enumerate((inverse_mean, scale, 1.0 / scale)):
            column = jnp.transpose(jnp.broadcast_to(value, (LANES, n_rows)))
            cols[index, i] = column.reshape(n_z, CORES, piece, LANES)

    take(me)

    def scale_frames(src, src_index, dst_index, first_lane, q, index):
        @pl.loop(0, piece // small)
        def _(i):
            at = pl.ds(i * small, small)
            for c in range(CORES):
                inverse = cols[index, 0, q, c, at, :]
                for g in range(0, half, LANES):
                    weight = weights[0:1, pl.ds(pl.multiple_of(first_lane + g, LANES), LANES)]
                    frame = src[src_index, q, c, at, g:g + LANES].astype(F32) * weight
                    frames_s[dst_index, q, c, at, g:g + LANES] = (frame * inverse).astype(BF16)

    for h in range(2):
        @pl.loop(0, n_z)
        def _(q):
            scale_frames(own, h, h, h * half, q, me)

    def product(k, pairs, row_block, col_block):
        other = 1 - core

        def at(n):
            return pl.ds(pl.multiple_of(n * pair, LANES), pair)

        def core_copy(n):
            return remote(
                core_out.at[k, :, :, at(n)], core_in.at[k, :, :, at(n)],
                core_send.at[k, n], core_recv.at[k, n], {"pix": z * CORES + other},
            )

        def tile(side, n):
            out = None
            for left, right in pairs:
                term = dot_rows(
                    frames_s[left, :, side].reshape(n_z * piece, half),
                    frames_s[right, n].reshape(pair, half),
                )
                out = term if out is None else out + term
            return out.reshape(n_z, piece, pair)

        @pl.loop(0, n_z)
        def _(n):
            core_out[k, :, :, at(n)] = tile(other, n)
            core_copy(n).start()

        @pl.loop(0, n_z)
        def _(n):
            value = tile(core, n)
            core_copy(n).wait()
            value = value + core_in[k, :, :, at(n)]
            value = value * widened(cols[row_block, 1, :, core], pair)
            acc[k, :, :, at(n)] = value * rows[col_block, 0:1, at(n)]

    def z_base(s):
        return n_z - (n_z >> s)

    def z_copy(k, s, m):
        bit = 1 << s
        sign = 1 - 2 * lax.rem(z // bit, 2)
        at = z_base(s) + m
        return remote(
            z_out.at[k, at], z_in.at[k, at], z_send.at[k, at], z_recv.at[k, at],
            {"pix": (z + sign * bit) * CORES + core},
        )

    def z_send_stage(k, s):
        bit = 1 << s
        low, top = lax.rem(z, bit), lax.rem(z // bit, 2)
        for m in range(n_z >> (s + 1)):
            j = m * 2 * bit + (1 - top) * bit + low
            z_out[k, z_base(s) + m] = quantized(acc[k, j])
            z_copy(k, s, m).start()

    def z_recv_stage(k, s):
        bit = 1 << s
        for m in range(n_z >> (s + 1)):
            z_copy(k, s, m).wait()
            j = m * 2 * bit + lax.rem(z, 2 * bit)
            acc[k, j] = acc[k, j] + restored(z_in[k, z_base(s) + m])

    product(0, ((0, 0), (1, 1)), me, me)
    for s in range(stages):
        z_send_stage(0, s)
        z_recv_stage(0, s)
    inverse_total = 1.0 / jnp.full((1, 1), pixel_total, F32)
    diag_ref[...] = acc[0, z] * widened(cols[me, 2, z, core], n_rows) * (rows[me, 1:2, :] * inverse_total)

    if square:
        for d in range(1, 4):
            tot_from(d).wait_recv()
        for d in range(1, 4):
            take(lax.rem(block + d, 4))
    else:
        @pl.when(has_prev)
        def _():
            tot_next().wait_recv()
            take(1)

    for q in range(n_z):
        for slot, which, target, _, arrives in streams:
            @pl.when(arrives)
            def _(slot=slot, which=which, target=target):
                data(slot, which, target, q).wait_recv()
                source = (across if slot == 0 else up) if square else 1
                scale_frames(frames_s, 2 + slot, 2 + slot, (x if square else slot) * half, q, source)

    if square:
        later, sooner = jnp.maximum(block, across), jnp.minimum(block, across)
        product(1, ((jnp.where(x == 0, 2, 1), jnp.where(x == 0, 0, 2)),), later, sooner)

        @pl.when(outer)
        def _():
            product(2, ((jnp.where(x == 0, 3, 2), jnp.where(x == 0, 2, 3)),), 2, 1)

        for s in range(stages):
            z_send_stage(1, s)

            @pl.when(outer)
            def _():
                z_send_stage(2, s)

            z_recv_stage(1, s)

            @pl.when(outer)
            def _():
                z_recv_stage(2, s)

        even = x == 0

        def last(source, slot, target):
            return remote(last_out.at[source], last_in.at[slot], last_send.at[source], last_recv.at[slot], {"frames": target})

        @pl.when(even)
        def _():
            last_out[0] = quantized(acc[1, z])
            last(0, 0, across).start()

        @pl.when(block == 0)
        def _():
            last_out[1] = quantized(acc[2, z])
            last(1, 1, up).start()

        @pl.when(block == 3)
        def _():
            last_out[1] = quantized(acc[2, z])
            last(1, 0, across).start()

        @pl.when(block == 0)
        def _():
            off_ref[...] = jnp.zeros_like(off_ref)

        def write(value):
            off_ref[...] = value * widened(cols[block, 2, z, core], n_rows) * (rows[before, 1:2, :] * inverse_total)

        @pl.when(x == 1)
        def _():
            last(0, 0, across).wait_recv()
            write(acc[1, z] + restored(last_in[0]))

        @pl.when(block == 2)
        def _():
            last(0, 0, across).wait_recv()
            last(1, 1, up).wait_recv()
            write(restored(last_in[0]) + restored(last_in[1]))

        @pl.when(even)
        def _():
            last(0, 0, across).wait_send()

        @pl.when(outer)
        def _():
            last(1, 1, up).wait_send()
    else:
        @pl.when(has_prev)
        def _():
            product(1, ((0, 2), (1, 3)), 0, 1)
            for s in range(stages):
                z_send_stage(1, s)
                z_recv_stage(1, s)
            off_ref[...] = acc[1, z] * widened(cols[0, 2, z, core], n_rows) * (rows[1, 1:2, :] * inverse_total)

        @pl.when(jnp.logical_not(has_prev))
        def _():
            off_ref[...] = jnp.zeros_like(off_ref)

    for d in range(1, n_pix):
        stat(d).wait_send()
    if square:
        for d in range(1, 4):
            tot(d).wait_send()
    else:
        @pl.when(has_next)
        def _():
            tot_next().wait_send()
    for q in range(n_z):
        for slot, which, target, sends, _ in streams:
            @pl.when(sends)
            def _(slot=slot, which=which, target=target):
                data(slot, which, target, q).wait_send()


def on_device(n_frames, n_pix, photon_counts, flat_field, owner_counts):
    n_rows, n_slots = photon_counts.shape
    half, piece, n_z = n_slots // 2, n_rows // n_pix, n_pix // CORES
    tiles, blocks = (3, 4) if n_frames == 4 else (2, 2)
    sent = max(n_z - 1, 1)
    flat = flat_field[None, :]
    out = jax.ShapeDtypeStruct((piece, n_rows), F32)
    dma = pltpu.SemaphoreType.DMA
    return pl.pallas_call(
        functools.partial(kernel, n_frames, n_pix),
        out_shape=(out, out),
        in_specs=[
            pl.BlockSpec(memory_space=pltpu.SMEM),
            pl.BlockSpec(memory_space=pl.ANY),
            pl.BlockSpec(memory_space=pltpu.VMEM),
        ],
        out_specs=(pl.BlockSpec(memory_space=pltpu.VMEM),) * 2,
        scratch_shapes=[
            pltpu.VMEM((n_rows, n_slots), jnp.int32),
            pltpu.VMEM((2, n_z, CORES, piece, half), BF16),
            pltpu.VMEM((4, n_z, CORES, piece, half), BF16),
            pltpu.VMEM((2, LANES, n_slots), BF16),
            pltpu.VMEM((16, n_slots), F32),
            pltpu.VMEM((n_pix, 8, n_rows), F32),
            pltpu.VMEM((blocks, 8, n_rows), F32),
            pltpu.VMEM((blocks, 8, n_rows), F32),
            pltpu.VMEM((blocks, 3, n_z, CORES, piece, LANES), F32),
            pltpu.VMEM((tiles, n_z, piece, n_rows), F32),
            pltpu.VMEM((tiles, n_z, piece, n_rows), F32),
            pltpu.VMEM((tiles, n_z, piece, n_rows), F32),
            pltpu.VMEM((tiles, sent, piece, n_rows), jnp.int16),
            pltpu.VMEM((tiles, sent, piece, n_rows), jnp.int16),
            pltpu.VMEM((2, piece, n_rows), jnp.int16),
            pltpu.VMEM((2, piece, n_rows), jnp.int16),
            dma((n_z,)),
            dma((2, n_z)), dma((2, n_z)),
            dma((n_pix,)), dma((n_pix,)),
            dma((4,)), dma((4,)),
            dma((tiles, n_z)), dma((tiles, n_z)),
            dma((tiles, sent)), dma((tiles, sent)),
            dma((2,)), dma((2,)),
        ],
        compiler_params=pltpu.CompilerParams(
            collective_id=0, has_side_effects=True, vmem_limit_bytes=62 * 1024 * 1024
        ),
        cost_estimate=pl.CostEstimate(
            flops=4 * n_rows * n_rows * n_slots, bytes_accessed=4 * n_rows * n_slots, transcendentals=0
        ),
    )(owner_counts, photon_counts, flat)


def solution(mesh):
    return jax.shard_map(
        functools.partial(on_device, mesh.shape["frames"], mesh.shape["pix"]),
        mesh=mesh,
        in_specs=(P("frames", "pix"), P("pix"), P()),
        out_specs=(P(("frames", "pix"), None), P(("frames", "pix"), None)),
        check_vma=False,
    )
```

```python
import functools

import jax
import jax.numpy as jnp
from jax import lax
from jax.experimental import pallas as pl
from jax.experimental.pallas import tpu as pltpu
from jax.sharding import PartitionSpec as P

MESH = pl.DeviceIdType.MESH
F32, BF16 = jnp.float32, jnp.bfloat16
LANES = 128
LEVELS = 64000.0
OFFSET = 32768
CORES = 2


def dot_rows(left, right):
    return lax.dot_general(left, right, (((1,), (1,)), ((), ())), preferred_element_type=F32)


def widened(column, lanes):
    count = lanes // LANES
    return column if count == 1 else jnp.concatenate([column] * count, axis=-1)


def quantized(value):
    return ((value + 0.5).astype(jnp.int32) - OFFSET).astype(jnp.int16)


def restored(value):
    return (value.astype(jnp.int32) + OFFSET).astype(F32)


def remote(src, dst, send_sem, recv_sem, device):
    return pltpu.make_async_remote_copy(
        src_ref=src, dst_ref=dst, send_sem=send_sem, recv_sem=recv_sem,
        device_id=device, device_id_type=MESH,
    )


def kernel(
    n_frames, n_pix,
    owner_ref, counts_hbm, flat_ref, diag_ref, off_ref,
    counts, own, frames_s, sum_rows, weights, stats, totals, rows, cols,
    core_out, core_in, acc, z_out, z_in, last_out, last_in,
    load_sem, data_send, data_recv, stat_send, stat_recv, tot_send, tot_recv,
    core_send, core_recv, z_send, z_recv, last_send, last_recv,
):
    square = n_frames == 4
    n_z = n_pix // CORES
    stages = n_z.bit_length() - 1
    block = lax.axis_index("frames")
    pix = lax.axis_index("pix")
    z, core = pix // CORES, lax.rem(pix, CORES)
    n_rows, n_slots = counts.shape
    half = n_slots // 2
    piece = n_rows // n_pix
    pair = CORES * piece
    x = lax.rem(block, 2)
    outer = jnp.logical_or(block == 0, block == 3)
    inner = jnp.logical_not(outer)
    across = block + 1 - 2 * x
    up = lax.rem(block + 2, 4)
    me = block if square else 0
    has_next, has_prev = block < n_frames - 1, block > 0
    follow = jnp.minimum(block + 1, n_frames - 1)
    before = jnp.maximum(block - 1, 0)

    def load(q):
        part = pl.ds(q * pair, pair)
        return pltpu.make_async_copy(counts_hbm.at[part], counts.at[part], load_sem.at[q])

    for q in range(n_z):
        load(q).start()

    barrier = pltpu.get_barrier_semaphore()
    for d in range(1, n_pix):
        pl.semaphore_signal(barrier, inc=1, device_id={"pix": lax.rem(pix + d, n_pix)}, device_id_type=MESH)
    if square:
        for d in range(1, 4):
            pl.semaphore_signal(barrier, inc=1, device_id={"frames": lax.rem(block + d, 4)}, device_id_type=MESH)
        pl.semaphore_wait(barrier, n_pix - 1 + 3)
    else:
        @pl.when(has_next)
        def _():
            pl.semaphore_signal(barrier, inc=1, device_id={"frames": follow}, device_id_type=MESH)

        @pl.when(has_prev)
        def _():
            pl.semaphore_signal(barrier, inc=1, device_id={"frames": before}, device_id_type=MESH)

        pl.semaphore_wait(barrier, n_pix - 1 + has_next.astype(jnp.int32) + has_prev.astype(jnp.int32))

    if square:
        always = block >= 0
        streams = ((0, 1 - x, across, always, always), (1, x, up, inner, outer))
    else:
        streams = ((0, 0, follow, has_next, has_prev), (1, 1, follow, has_next, has_prev))

    def data(slot, which, target, q):
        return remote(
            own.at[which, q], frames_s.at[2 + slot, q],
            data_send.at[slot, q], data_recv.at[slot, q], {"frames": target},
        )

    pixel_total = owner_ref[0]
    for i in range(1, n_pix):
        pixel_total = pixel_total + owner_ref[i]
    pixel_total = pixel_total.astype(F32)
    limit = owner_ref[pix]
    slot_ids = lax.broadcasted_iota(jnp.int32, (16, n_slots), 1)
    valid = (slot_ids < limit).astype(F32)
    weight = flat_ref[...] * valid
    weights[...] = weight
    first = weight.astype(BF16).astype(F32)
    second = (weight - first).astype(BF16).astype(F32)
    third = weight - first - second
    line = lax.broadcasted_iota(jnp.int32, (16, n_slots), 0)
    none = jnp.zeros_like(weight)
    split = jnp.where(line == 0, first, jnp.where(line == 1, second, jnp.where(line == 2, third, none)))
    filler = jnp.zeros((LANES - 16, n_slots), BF16)
    for i, value in enumerate((split, jnp.where(line == 3, weight * weight, none))):
        sum_rows[i, 0:16, :] = value.astype(BF16)
        sum_rows[i, 16:LANES, :] = filler

    stats[pix] = jnp.zeros((8, n_rows), F32)
    small = 16
    for q in range(n_z):
        load(q).wait()

        @pl.loop(0, piece // small)
        def _(i):
            for c in range(CORES):
                for h in range(2):
                    taken = counts[pl.ds(q * pair + c * piece + i * small, small), h * half:(h + 1) * half]
                    own[h, q, c, pl.ds(i * small, small), :] = taken.astype(F32).astype(BF16)

        for slot, which, target, sends, _ in streams:
            @pl.when(sends)
            def _(slot=slot, which=which, target=target):
                data(slot, which, target, q).start()

    for q in range(n_z):
        sums = jnp.zeros((pair, LANES), F32)
        for h in range(2):
            held = own[h, q].reshape(pair, half)
            lanes = slice(h * half, (h + 1) * half)
            sums = sums + dot_rows(held, sum_rows[0, :, lanes]) + dot_rows(held * held, sum_rows[1, :, lanes])
        sums = jnp.transpose(sums)
        part = slice(q * pair, (q + 1) * pair)
        stats[pix, 0:1, part] = sums[0:1] + sums[1:2] + sums[2:3]
        stats[pix, 1:2, part] = sums[3:4]

    def stat(d):
        return remote(
            stats.at[pix], stats.at[pix], stat_send.at[d], stat_recv.at[pix],
            {"pix": lax.rem(pix + d, n_pix)},
        )

    def stat_from(d):
        source = lax.rem(pix + d, n_pix)
        return remote(stats.at[source], stats.at[source], stat_send.at[d], stat_recv.at[source], {"pix": source})

    for d in range(1, n_pix):
        stat(d).start()
    for d in range(1, n_pix):
        stat_from(d).wait_recv()
    total = stats[0]
    for i in range(1, n_pix):
        total = total + stats[i]
    totals[me] = total

    if square:
        def tot(d):
            return remote(totals.at[me], totals.at[me], tot_send.at[d], tot_recv.at[me], {"frames": lax.rem(block + d, 4)})

        def tot_from(d):
            source = lax.rem(block + d, 4)
            return remote(totals.at[source], totals.at[source], tot_send.at[d], tot_recv.at[source], {"frames": source})

        for d in range(1, 4):
            tot(d).start()
    else:
        def tot_next():
            return remote(totals.at[0], totals.at[1], tot_send.at[0], tot_recv.at[0], {"frames": follow})

        @pl.when(has_next)
        def _():
            tot_next().start()

    def take(index):
        held = totals[index]
        inverse_mean = pixel_total / held[0:1]
        norm = jnp.sqrt(held[1:2]) * inverse_mean
        scale = LEVELS ** 0.5 / norm
        rows[index, 0:1, :] = scale
        rows[index, 1:2, :] = 1.0 / scale
        for i, value in enumerate((inverse_mean, scale, 1.0 / scale)):
            column = jnp.transpose(jnp.broadcast_to(value, (LANES, n_rows)))
            cols[index, i] = column.reshape(n_z, CORES, piece, LANES)

    take(me)

    def scale_frames(src, src_index, dst_index, first_lane, q, index):
        @pl.loop(0, piece // small)
        def _(i):
            at = pl.ds(i * small, small)
            for c in range(CORES):
                inverse = cols[index, 0, q, c, at, :]
                for g in range(0, half, LANES):
                    weight = weights[0:1, pl.ds(pl.multiple_of(first_lane + g, LANES), LANES)]
                    frame = src[src_index, q, c, at, g:g + LANES].astype(F32) * weight
                    frames_s[dst_index, q, c, at, g:g + LANES] = (frame * inverse).astype(BF16)

    for h in range(2):
        @pl.loop(0, n_z)
        def _(q):
            scale_frames(own, h, h, h * half, q, me)

    def product(k, pairs, row_block, col_block):
        other = 1 - core

        def at(n):
            return pl.ds(pl.multiple_of(n * pair, LANES), pair)

        def core_copy(n):
            return remote(
                core_out.at[k, :, :, at(n)], core_in.at[k, :, :, at(n)],
                core_send.at[k, n], core_recv.at[k, n], {"pix": z * CORES + other},
            )

        def tile(side, n):
            out = None
            for left, right in pairs:
                term = dot_rows(
                    frames_s[left, :, side].reshape(n_z * piece, half),
                    frames_s[right, n].reshape(pair, half),
                )
                out = term if out is None else out + term
            return out.reshape(n_z, piece, pair)

        @pl.loop(0, n_z)
        def _(n):
            core_out[k, :, :, at(n)] = tile(other, n)
            core_copy(n).start()

        @pl.loop(0, n_z)
        def _(n):
            value = tile(core, n)
            core_copy(n).wait()
            value = value + core_in[k, :, :, at(n)]
            value = value * widened(cols[row_block, 1, :, core], pair)
            acc[k, :, :, at(n)] = value * rows[col_block, 0:1, at(n)]

    def z_base(s):
        return n_z - (n_z >> s)

    def z_copy(k, s, m):
        bit = 1 << s
        sign = 1 - 2 * lax.rem(z // bit, 2)
        at = z_base(s) + m
        return remote(
            z_out.at[k, at], z_in.at[k, at], z_send.at[k, at], z_recv.at[k, at],
            {"pix": (z + sign * bit) * CORES + core},
        )

    def z_send_stage(k, s):
        bit = 1 << s
        low, top = lax.rem(z, bit), lax.rem(z // bit, 2)
        for m in range(n_z >> (s + 1)):
            j = m * 2 * bit + (1 - top) * bit + low
            z_out[k, z_base(s) + m] = quantized(acc[k, j])
            z_copy(k, s, m).start()

    def z_recv_stage(k, s):
        bit = 1 << s
        for m in range(n_z >> (s + 1)):
            z_copy(k, s, m).wait()
            j = m * 2 * bit + lax.rem(z, 2 * bit)
            acc[k, j] = acc[k, j] + restored(z_in[k, z_base(s) + m])

    def diag_steps(first_stage, end_stage):
        for s in range(max(first_stage, 0), end_stage):
            z_recv_stage(0, s)
            if s + 1 < stages:
                z_send_stage(0, s + 1)

    def finish_diag():
        diag_steps(stages - 1, stages)
        diag_ref[...] = acc[0, z] * widened(cols[me, 2, z, core], n_rows) * (rows[me, 1:2, :] * inverse_total)

    def receive(q):
        for slot, which, target, _, arrives in streams:
            @pl.when(arrives)
            def _(slot=slot, which=which, target=target):
                data(slot, which, target, q).wait_recv()
                source = (across if slot == 0 else up) if square else 1
                scale_frames(frames_s, 2 + slot, 2 + slot, (x if square else slot) * half, q, source)

    inverse_total = 1.0 / jnp.full((1, 1), pixel_total, F32)
    product(0, ((0, 0), (1, 1)), me, me)
    if stages:
        z_send_stage(0, 0)

    if square:
        for d in range(1, 4):
            tot_from(d).wait_recv()
        for d in range(1, 4):
            take(lax.rem(block + d, 4))
    else:
        @pl.when(has_prev)
        def _():
            tot_next().wait_recv()
            take(1)

    for q in range(n_z - 1):
        receive(q)
    diag_steps(0, stages - 1)
    receive(n_z - 1)

    if square:
        even = x == 0
        later, sooner = jnp.maximum(block, across), jnp.minimum(block, across)

        def last(source, slot, target):
            return remote(last_out.at[source], last_in.at[slot], last_send.at[source], last_recv.at[slot], {"frames": target})

        def send_last(k):
            if k == 1:
                @pl.when(even)
                def _():
                    last_out[0] = quantized(acc[1, z])
                    last(0, 0, across).start()
            else:
                last_out[1] = quantized(acc[2, z])

                @pl.when(block == 0)
                def _():
                    last(1, 1, up).start()

                @pl.when(block == 3)
                def _():
                    last(1, 0, across).start()

        def advance(k, s):
            if s >= 0:
                z_recv_stage(k, s)
            if s + 1 < stages:
                z_send_stage(k, s + 1)
            else:
                send_last(k)

        product(1, ((jnp.where(even, 2, 1), jnp.where(even, 0, 2)),), later, sooner)
        advance(1, -1)

        @pl.when(outer)
        def _():
            product(2, ((jnp.where(even, 3, 2), jnp.where(even, 2, 3)),), 2, 1)
            advance(2, -1)

        finish_diag()
        for s in range(stages):
            advance(1, s)

            @pl.when(outer)
            def _(s=s):
                advance(2, s)

        def write(value):
            off_ref[...] = value * widened(cols[block, 2, z, core], n_rows) * (rows[before, 1:2, :] * inverse_total)

        @pl.when(block == 0)
        def _():
            off_ref[...] = jnp.zeros_like(off_ref)

        @pl.when(x == 1)
        def _():
            last(0, 0, across).wait_recv()
            write(acc[1, z] + restored(last_in[0]))

        @pl.when(block == 2)
        def _():
            last(0, 0, across).wait_recv()
            last(1, 1, up).wait_recv()
            write(restored(last_in[0]) + restored(last_in[1]))

        @pl.when(even)
        def _():
            last(0, 0, across).wait_send()

        @pl.when(outer)
        def _():
            last(1, 1, up).wait_send()
    else:
        @pl.when(has_prev)
        def _():
            product(1, ((0, 2), (1, 3)), 0, 1)
            for s in range(stages):
                z_send_stage(1, s)
                z_recv_stage(1, s)
            off_ref[...] = acc[1, z] * widened(cols[0, 2, z, core], n_rows) * (rows[1, 1:2, :] * inverse_total)

        @pl.when(jnp.logical_not(has_prev))
        def _():
            off_ref[...] = jnp.zeros_like(off_ref)

        finish_diag()

    for d in range(1, n_pix):
        stat(d).wait_send()
    if square:
        for d in range(1, 4):
            tot(d).wait_send()
    else:
        @pl.when(has_next)
        def _():
            tot_next().wait_send()
    for q in range(n_z):
        for slot, which, target, sends, _ in streams:
            @pl.when(sends)
            def _(slot=slot, which=which, target=target):
                data(slot, which, target, q).wait_send()


def on_device(n_frames, n_pix, photon_counts, flat_field, owner_counts):
    n_rows, n_slots = photon_counts.shape
    half, piece, n_z = n_slots // 2, n_rows // n_pix, n_pix // CORES
    tiles, blocks = (3, 4) if n_frames == 4 else (2, 2)
    sent = max(n_z - 1, 1)
    flat = flat_field[None, :]
    out = jax.ShapeDtypeStruct((piece, n_rows), F32)
    dma = pltpu.SemaphoreType.DMA
    return pl.pallas_call(
        functools.partial(kernel, n_frames, n_pix),
        out_shape=(out, out),
        in_specs=[
            pl.BlockSpec(memory_space=pltpu.SMEM),
            pl.BlockSpec(memory_space=pl.ANY),
            pl.BlockSpec(memory_space=pltpu.VMEM),
        ],
        out_specs=(pl.BlockSpec(memory_space=pltpu.VMEM),) * 2,
        scratch_shapes=[
            pltpu.VMEM((n_rows, n_slots), jnp.int32),
            pltpu.VMEM((2, n_z, CORES, piece, half), BF16),
            pltpu.VMEM((4, n_z, CORES, piece, half), BF16),
            pltpu.VMEM((2, LANES, n_slots), BF16),
            pltpu.VMEM((16, n_slots), F32),
            pltpu.VMEM((n_pix, 8, n_rows), F32),
            pltpu.VMEM((blocks, 8, n_rows), F32),
            pltpu.VMEM((blocks, 8, n_rows), F32),
            pltpu.VMEM((blocks, 3, n_z, CORES, piece, LANES), F32),
            pltpu.VMEM((tiles, n_z, piece, n_rows), F32),
            pltpu.VMEM((tiles, n_z, piece, n_rows), F32),
            pltpu.VMEM((tiles, n_z, piece, n_rows), F32),
            pltpu.VMEM((tiles, sent, piece, n_rows), jnp.int16),
            pltpu.VMEM((tiles, sent, piece, n_rows), jnp.int16),
            pltpu.VMEM((2, piece, n_rows), jnp.int16),
            pltpu.VMEM((2, piece, n_rows), jnp.int16),
            dma((n_z,)),
            dma((2, n_z)), dma((2, n_z)),
            dma((n_pix,)), dma((n_pix,)),
            dma((4,)), dma((4,)),
            dma((tiles, n_z)), dma((tiles, n_z)),
            dma((tiles, sent)), dma((tiles, sent)),
            dma((2,)), dma((2,)),
        ],
        compiler_params=pltpu.CompilerParams(
            collective_id=0, has_side_effects=True, vmem_limit_bytes=62 * 1024 * 1024
        ),
        cost_estimate=pl.CostEstimate(
            flops=4 * n_rows * n_rows * n_slots, bytes_accessed=4 * n_rows * n_slots, transcendentals=0
        ),
    )(owner_counts, photon_counts, flat)


def solution(mesh):
    return jax.shard_map(
        functools.partial(on_device, mesh.shape["frames"], mesh.shape["pix"]),
        mesh=mesh,
        in_specs=(P("frames", "pix"), P("pix"), P()),
        out_specs=(P(("frames", "pix"), None), P(("frames", "pix"), None)),
        check_vma=False,
    )
```

```python
import functools

import jax
import jax.numpy as jnp
from jax import lax
from jax.experimental import pallas as pl
from jax.experimental.pallas import tpu as pltpu
from jax.sharding import PartitionSpec as P

MESH = pl.DeviceIdType.MESH
F32, BF16 = jnp.float32, jnp.bfloat16
LANES = 128
LEVELS = 64000.0
OFFSET = 32768
CORES = 2


def dot_rows(left, right):
    return lax.dot_general(left, right, (((1,), (1,)), ((), ())), preferred_element_type=F32)


def widened(column, lanes):
    count = lanes // LANES
    return column if count == 1 else jnp.concatenate([column] * count, axis=-1)


def quantized(value):
    return ((value + 0.5).astype(jnp.int32) - OFFSET).astype(jnp.int16)


def restored(value):
    return (value.astype(jnp.int32) + OFFSET).astype(F32)


def remote(src, dst, send_sem, recv_sem, device):
    return pltpu.make_async_remote_copy(
        src_ref=src, dst_ref=dst, send_sem=send_sem, recv_sem=recv_sem,
        device_id=device, device_id_type=MESH,
    )


def kernel(
    n_frames, n_pix,
    owner_ref, counts_hbm, flat_ref, diag_ref, off_ref,
    counts, own, frames_s, sum_rows, weights, stats, totals, rows, cols,
    prod, core_in, z_out, z_in, last_out, last_in,
    load_sem, data_send, data_recv, stat_send, stat_recv, tot_send, tot_recv,
    core_send, core_recv, z_send, z_recv, last_send, last_recv,
):
    square = n_frames == 4
    n_z = n_pix // CORES
    stages = n_z.bit_length() - 1
    block = lax.axis_index("frames")
    pix = lax.axis_index("pix")
    z, core = pix // CORES, lax.rem(pix, CORES)
    n_rows, n_slots = counts.shape
    half = n_slots // 2
    piece = n_rows // n_pix
    pair = CORES * piece
    x = lax.rem(block, 2)
    outer = jnp.logical_or(block == 0, block == 3)
    inner = jnp.logical_not(outer)
    across = block + 1 - 2 * x
    up = lax.rem(block + 2, 4)
    me = block if square else 0
    has_next, has_prev = block < n_frames - 1, block > 0
    follow = jnp.minimum(block + 1, n_frames - 1)
    before = jnp.maximum(block - 1, 0)

    def load(q):
        part = pl.ds(q * pair, pair)
        return pltpu.make_async_copy(counts_hbm.at[part], counts.at[part], load_sem.at[q])

    for q in range(n_z):
        load(q).start()

    barrier = pltpu.get_barrier_semaphore()
    for d in range(1, n_pix):
        pl.semaphore_signal(barrier, inc=1, device_id={"pix": lax.rem(pix + d, n_pix)}, device_id_type=MESH)
    if square:
        for d in range(1, 4):
            pl.semaphore_signal(barrier, inc=1, device_id={"frames": lax.rem(block + d, 4)}, device_id_type=MESH)
        pl.semaphore_wait(barrier, n_pix - 1 + 3)
    else:
        @pl.when(has_next)
        def _():
            pl.semaphore_signal(barrier, inc=1, device_id={"frames": follow}, device_id_type=MESH)

        @pl.when(has_prev)
        def _():
            pl.semaphore_signal(barrier, inc=1, device_id={"frames": before}, device_id_type=MESH)

        pl.semaphore_wait(barrier, n_pix - 1 + has_next.astype(jnp.int32) + has_prev.astype(jnp.int32))

    if square:
        always = block >= 0
        streams = ((0, 1 - x, across, always, always), (1, x, up, inner, outer))
    else:
        streams = ((0, 0, follow, has_next, has_prev), (1, 1, follow, has_next, has_prev))

    def data(slot, which, target, q):
        return remote(
            own.at[which, q], frames_s.at[2 + slot, q],
            data_send.at[slot, q], data_recv.at[slot, q], {"frames": target},
        )

    pixel_total = owner_ref[0]
    for i in range(1, n_pix):
        pixel_total = pixel_total + owner_ref[i]
    pixel_total = pixel_total.astype(F32)
    limit = owner_ref[pix]
    slot_ids = lax.broadcasted_iota(jnp.int32, (16, n_slots), 1)
    valid = (slot_ids < limit).astype(F32)
    weight = flat_ref[...] * valid
    weights[...] = weight
    first = weight.astype(BF16).astype(F32)
    second = (weight - first).astype(BF16).astype(F32)
    third = weight - first - second
    line = lax.broadcasted_iota(jnp.int32, (16, n_slots), 0)
    none = jnp.zeros_like(weight)
    split = jnp.where(line == 0, first, jnp.where(line == 1, second, jnp.where(line == 2, third, none)))
    filler = jnp.zeros((LANES - 16, n_slots), BF16)
    for i, value in enumerate((split, jnp.where(line == 3, weight * weight, none))):
        sum_rows[i, 0:16, :] = value.astype(BF16)
        sum_rows[i, 16:LANES, :] = filler

    stats[pix] = jnp.zeros((8, n_rows), F32)
    small = 16
    for q in range(n_z):
        load(q).wait()

        @pl.loop(0, piece // small)
        def _(i):
            for c in range(CORES):
                for h in range(2):
                    taken = counts[pl.ds(q * pair + c * piece + i * small, small), h * half:(h + 1) * half]
                    own[h, q, c, pl.ds(i * small, small), :] = taken.astype(F32).astype(BF16)

        for slot, which, target, sends, _ in streams:
            @pl.when(sends)
            def _(slot=slot, which=which, target=target):
                data(slot, which, target, q).start()

    for q in range(n_z):
        sums = jnp.zeros((pair, LANES), F32)
        for h in range(2):
            held = own[h, q].reshape(pair, half)
            lanes = slice(h * half, (h + 1) * half)
            sums = sums + dot_rows(held, sum_rows[0, :, lanes]) + dot_rows(held * held, sum_rows[1, :, lanes])
        sums = jnp.transpose(sums)
        part = slice(q * pair, (q + 1) * pair)
        stats[pix, 0:1, part] = sums[0:1] + sums[1:2] + sums[2:3]
        stats[pix, 1:2, part] = sums[3:4]

    def stat(d):
        return remote(
            stats.at[pix], stats.at[pix], stat_send.at[d], stat_recv.at[pix],
            {"pix": lax.rem(pix + d, n_pix)},
        )

    def stat_from(d):
        source = lax.rem(pix + d, n_pix)
        return remote(stats.at[source], stats.at[source], stat_send.at[d], stat_recv.at[source], {"pix": source})

    for d in range(1, n_pix):
        stat(d).start()
    for d in range(1, n_pix):
        stat_from(d).wait_recv()
    total = stats[0]
    for i in range(1, n_pix):
        total = total + stats[i]
    totals[me] = total

    if square:
        def tot(d):
            return remote(totals.at[me], totals.at[me], tot_send.at[d], tot_recv.at[me], {"frames": lax.rem(block + d, 4)})

        def tot_from(d):
            source = lax.rem(block + d, 4)
            return remote(totals.at[source], totals.at[source], tot_send.at[d], tot_recv.at[source], {"frames": source})

        for d in range(1, 4):
            tot(d).start()
    else:
        def tot_next():
            return remote(totals.at[0], totals.at[1], tot_send.at[0], tot_recv.at[0], {"frames": follow})

        @pl.when(has_next)
        def _():
            tot_next().start()

    def take(index):
        held = totals[index]
        inverse_mean = pixel_total / held[0:1]
        norm = jnp.sqrt(held[1:2]) * inverse_mean
        scale = LEVELS ** 0.5 / norm
        rows[index, 0:1, :] = scale
        rows[index, 1:2, :] = 1.0 / scale
        for i, value in enumerate((inverse_mean, scale, 1.0 / scale)):
            column = jnp.transpose(jnp.broadcast_to(value, (LANES, n_rows)))
            cols[index, i] = column.reshape(n_z, CORES, piece, LANES)

    take(me)

    def scale_frames(src, src_index, dst_index, first_lane, q, index):
        @pl.loop(0, piece // small)
        def _(i):
            at = pl.ds(i * small, small)
            for c in range(CORES):
                inverse = cols[index, 0, q, c, at, :]
                for g in range(0, half, LANES):
                    weight = weights[0:1, pl.ds(pl.multiple_of(first_lane + g, LANES), LANES)]
                    frame = src[src_index, q, c, at, g:g + LANES].astype(F32) * weight
                    frames_s[dst_index, q, c, at, g:g + LANES] = (frame * inverse).astype(BF16)

    for h in range(2):
        @pl.loop(0, n_z)
        def _(q):
            scale_frames(own, h, h, h * half, q, me)

    other = 1 - core
    everything = slice(None)

    def lanes_of(n):
        return pl.ds(n * pair, pair)

    def core_columns(k, n):
        return remote(
            prod.at[k, :, other, :, lanes_of(n)], core_in.at[k, :, :, lanes_of(n)],
            core_send.at[k, n], core_recv.at[k, n], {"pix": z * CORES + other},
        )

    def core_rows(k, j):
        return remote(
            prod.at[k, j, other], core_in.at[k, j],
            core_send.at[k, j], core_recv.at[k, j], {"pix": z * CORES + other},
        )

    def multiply_columns(k, pairs, n):
        out = None
        for left, right in pairs:
            term = dot_rows(frames_s[left].reshape(n_rows, half), frames_s[right, n].reshape(pair, half))
            out = term if out is None else out + term
        prod[k, :, :, :, lanes_of(n)] = out.reshape(n_z, CORES, piece, pair)
        core_columns(k, n).start()

    def merge_columns(k, n, row_block, col_block):
        core_columns(k, n).wait()
        value = prod[k, :, core, :, lanes_of(n)] + core_in[k, :, :, lanes_of(n)]
        value = value * widened(cols[row_block, 1, :, core], pair)
        prod[k, :, core, :, lanes_of(n)] = value * rows[col_block, 0:1, lanes_of(n)]

    def multiply_rows(k, left, right, j):
        for n in range(n_z):
            out = dot_rows(frames_s[left, j].reshape(pair, half), frames_s[right, n].reshape(pair, half))
            prod[k, j, :, :, lanes_of(n)] = out.reshape(CORES, piece, pair)
        core_rows(k, j).start()

    def merge_rows(k, j, row_block, col_block):
        core_rows(k, j).wait()
        value = (prod[k, j, core] + core_in[k, j]) * widened(cols[row_block, 1, j, core], n_rows)
        prod[k, j, core] = value * rows[col_block, 0:1, :]

    def product(k, pairs, row_block, col_block):
        for n in range(n_z):
            multiply_columns(k, pairs, n)
        for n in range(n_z):
            merge_columns(k, n, row_block, col_block)

    def z_copy(k, s, m, part, c):
        bit = 1 << s
        sign = 1 - 2 * lax.rem(z // bit, 2)
        at = n_z - (n_z >> s) + m
        return remote(
            z_out.at[k, at, :, part], z_in.at[k, at, :, part], z_send.at[k, at, c], z_recv.at[k, at, c],
            {"pix": (z + sign * bit) * CORES + core},
        )

    def z_put(k, s, m, part=everything, c=0):
        bit = 1 << s
        j = m * 2 * bit + (1 - lax.rem(z // bit, 2)) * bit + lax.rem(z, bit)
        z_out[k, n_z - (n_z >> s) + m, :, part] = quantized(prod[k, j, core, :, part])
        z_copy(k, s, m, part, c).start()

    def z_get(k, s, m, part=everything, c=0, both=True):
        bit = 1 << s
        copy = z_copy(k, s, m, part, c)
        copy.wait_recv()
        if both:
            copy.wait_send()
        j = m * 2 * bit + lax.rem(z, 2 * bit)
        prod[k, j, core, :, part] = prod[k, j, core, :, part] + restored(z_in[k, n_z - (n_z >> s) + m, :, part])

    def order(s):
        count = n_z >> (s + 1)
        if count == 1:
            return [0], []
        held = lax.rem(z // (2 << s), 2)
        return [2 * i + 1 - held for i in range(count // 2)], [2 * i + held for i in range(count // 2)]

    def advance(k, s, part=everything, c=0):
        ahead, after = order(s) if s >= 0 else ((), ())
        for m in ahead:
            z_get(k, s, m, part, c)
        if s + 1 < stages:
            for m in sum(order(s + 1), []):
                z_put(k, s + 1, m, part, c)
        for m in after:
            z_get(k, s, m, part, c)

    def at_stage(s, j, sends):
        bit = 1 << s
        same = lax.rem(z // bit, 2) == (j >> s) % 2
        return jnp.logical_and(lax.rem(z, bit) == j % bit, jnp.logical_not(same) if sends else same)

    def advance_rows(k, s, j):
        if s >= 0:
            @pl.when(at_stage(s, j, False))
            def _():
                z_get(k, s, j >> (s + 1), both=False)
        if s + 1 < stages:
            @pl.when(at_stage(s + 1, j, True))
            def _():
                z_put(k, s + 1, j >> (s + 2))

    def finish_diag():
        advance(0, stages - 1)
        diag_ref[...] = prod[0, z, core] * widened(cols[me, 2, z, core], n_rows) * (rows[me, 1:2, :] * inverse_total)

    def receive(q):
        for slot, which, target, _, arrives in streams:
            @pl.when(arrives)
            def _(slot=slot, which=which, target=target):
                data(slot, which, target, q).wait_recv()
                source = (across if slot == 0 else up) if square else 1
                scale_frames(frames_s, 2 + slot, 2 + slot, (x if square else slot) * half, q, source)

    inverse_total = 1.0 / jnp.full((1, 1), pixel_total, F32)
    product(0, ((0, 0), (1, 1)), me, me)
    advance(0, -1)

    if square:
        for d in range(1, 4):
            tot_from(d).wait_recv()
        for d in range(1, 4):
            take(lax.rem(block + d, 4))
    else:
        @pl.when(has_prev)
        def _():
            tot_next().wait_recv()
            take(1)

    if square:
        even = x == 0
        odd = x == 1

        def last(source, slot, target):
            return remote(last_out.at[source], last_in.at[slot], last_send.at[source], last_recv.at[slot], {"frames": target})

        def onward(q, s):
            @pl.when(even)
            def _():
                advance_rows(1, s, q)

            @pl.when(odd)
            def _():
                advance(1, s, lanes_of(q), q)

        for q in range(n_z):
            receive(q)

            @pl.when(even)
            def _():
                multiply_rows(1, 2, 0, q)

            @pl.when(odd)
            def _():
                multiply_columns(1, ((1, 2),), q)

            if q == n_z - 1:
                @pl.when(outer)
                def _():
                    for n in range(n_z):
                        multiply_columns(2, ((jnp.where(even, 3, 2), jnp.where(even, 2, 3)),), n)

            @pl.when(even)
            def _():
                merge_rows(1, q, across, block)

            @pl.when(odd)
            def _():
                merge_columns(1, q, block, across)

            onward(q, -1)
            for s in range(stages):
                if s < q:
                    onward(q - 1 - s, s)
            if q < stages - 1:
                advance(0, q)

        @pl.when(outer)
        def _():
            for n in range(n_z):
                merge_columns(2, n, 2, 1)
            advance(2, -1)

        remaining = [(q, s) for q in range(n_z) for s in range(max(n_z - 1 - q, 0), stages)]
        for q, s in remaining[:-1]:
            onward(q, s)

        @pl.when(outer)
        def _():
            for s in range(stages - 1):
                advance(2, s)

        for q, s in remaining[-1:]:
            onward(q, s)

        @pl.when(even)
        def _():
            last_out[0] = quantized(prod[1, z, core])
            last(0, 0, across).start()

        finish_diag()

        @pl.when(outer)
        def _():
            advance(2, stages - 1)
            last_out[1] = quantized(prod[2, z, core])

        @pl.when(block == 0)
        def _():
            last(1, 1, up).start()

        @pl.when(block == 3)
        def _():
            last(1, 0, across).start()

        def write(value):
            off_ref[...] = value * widened(cols[block, 2, z, core], n_rows) * (rows[before, 1:2, :] * inverse_total)

        @pl.when(block == 0)
        def _():
            off_ref[...] = jnp.zeros_like(off_ref)

        @pl.when(odd)
        def _():
            last(0, 0, across).wait_recv()
            write(prod[1, z, core] + restored(last_in[0]))

        @pl.when(block == 2)
        def _():
            last(0, 0, across).wait_recv()
            last(1, 1, up).wait_recv()
            write(restored(last_in[0]) + restored(last_in[1]))

        @pl.when(even)
        def _():
            last(0, 0, across).wait_send()
            for s in range(stages):
                for j in range(n_z):
                    @pl.when(at_stage(s, j, True))
                    def _(s=s, j=j):
                        z_copy(1, s, j >> (s + 1), everything, 0).wait_send()

        @pl.when(outer)
        def _():
            last(1, 1, up).wait_send()
    else:
        for s in range(stages - 1):
            advance(0, s)
        for q in range(n_z):
            receive(q)

        @pl.when(has_prev)
        def _():
            product(1, ((0, 2), (1, 3)), 0, 1)
            for s in range(-1, stages):
                advance(1, s)
            off_ref[...] = prod[1, z, core] * widened(cols[0, 2, z, core], n_rows) * (rows[1, 1:2, :] * inverse_total)

        @pl.when(jnp.logical_not(has_prev))
        def _():
            off_ref[...] = jnp.zeros_like(off_ref)

        finish_diag()

    for d in range(1, n_pix):
        stat(d).wait_send()
    if square:
        for d in range(1, 4):
            tot(d).wait_send()
    else:
        @pl.when(has_next)
        def _():
            tot_next().wait_send()
    for q in range(n_z):
        for slot, which, target, sends, _ in streams:
            @pl.when(sends)
            def _(slot=slot, which=which, target=target):
                data(slot, which, target, q).wait_send()


def on_device(n_frames, n_pix, photon_counts, flat_field, owner_counts):
    n_rows, n_slots = photon_counts.shape
    half, piece, n_z = n_slots // 2, n_rows // n_pix, n_pix // CORES
    tiles, blocks = (3, 4) if n_frames == 4 else (2, 2)
    sent = max(n_z - 1, 1)
    flat = flat_field[None, :]
    out = jax.ShapeDtypeStruct((piece, n_rows), F32)
    dma = pltpu.SemaphoreType.DMA
    return pl.pallas_call(
        functools.partial(kernel, n_frames, n_pix),
        out_shape=(out, out),
        in_specs=[
            pl.BlockSpec(memory_space=pltpu.SMEM),
            pl.BlockSpec(memory_space=pl.ANY),
            pl.BlockSpec(memory_space=pltpu.VMEM),
        ],
        out_specs=(pl.BlockSpec(memory_space=pltpu.VMEM),) * 2,
        scratch_shapes=[
            pltpu.VMEM((n_rows, n_slots), jnp.int32),
            pltpu.VMEM((2, n_z, CORES, piece, half), BF16),
            pltpu.VMEM((4, n_z, CORES, piece, half), BF16),
            pltpu.VMEM((2, LANES, n_slots), BF16),
            pltpu.VMEM((16, n_slots), F32),
            pltpu.VMEM((n_pix, 8, n_rows), F32),
            pltpu.VMEM((blocks, 8, n_rows), F32),
            pltpu.VMEM((blocks, 8, n_rows), F32),
            pltpu.VMEM((blocks, 3, n_z, CORES, piece, LANES), F32),
            pltpu.VMEM((tiles, n_z, CORES, piece, n_rows), F32),
            pltpu.VMEM((tiles, n_z, piece, n_rows), F32),
            pltpu.VMEM((tiles, sent, piece, n_rows), jnp.int16),
            pltpu.VMEM((tiles, sent, piece, n_rows), jnp.int16),
            pltpu.VMEM((2, piece, n_rows), jnp.int16),
            pltpu.VMEM((2, piece, n_rows), jnp.int16),
            dma((n_z,)),
            dma((2, n_z)), dma((2, n_z)),
            dma((n_pix,)), dma((n_pix,)),
            dma((4,)), dma((4,)),
            dma((tiles, n_z)), dma((tiles, n_z)),
            dma((tiles, sent, n_z)), dma((tiles, sent, n_z)),
            dma((2,)), dma((2,)),
        ],
        compiler_params=pltpu.CompilerParams(
            collective_id=0, has_side_effects=True, vmem_limit_bytes=62 * 1024 * 1024
        ),
        cost_estimate=pl.CostEstimate(
            flops=4 * n_rows * n_rows * n_slots, bytes_accessed=4 * n_rows * n_slots, transcendentals=0
        ),
    )(owner_counts, photon_counts, flat)


def solution(mesh):
    return jax.shard_map(
        functools.partial(on_device, mesh.shape["frames"], mesh.shape["pix"]),
        mesh=mesh,
        in_specs=(P("frames", "pix"), P("pix"), P()),
        out_specs=(P(("frames", "pix"), None), P(("frames", "pix"), None)),
        check_vma=False,
    )
```

```python
import functools

import jax
import jax.numpy as jnp
from jax import lax
from jax.experimental import pallas as pl
from jax.experimental.pallas import tpu as pltpu
from jax.sharding import PartitionSpec as P

MESH = pl.DeviceIdType.MESH
F32, BF16 = jnp.float32, jnp.bfloat16
LANES = 128
LEVELS = 64000.0
OFFSET = 32768
CORES = 2


def dot_rows(left, right):
    return lax.dot_general(left, right, (((1,), (1,)), ((), ())), preferred_element_type=F32)


def widened(column, lanes):
    count = lanes // LANES
    return column if count == 1 else jnp.concatenate([column] * count, axis=-1)


def quantized(value):
    return ((value + 0.5).astype(jnp.int32) - OFFSET).astype(jnp.int16)


def restored(value):
    return (value.astype(jnp.int32) + OFFSET).astype(F32)


def remote(src, dst, send_sem, recv_sem, device):
    return pltpu.make_async_remote_copy(
        src_ref=src, dst_ref=dst, send_sem=send_sem, recv_sem=recv_sem,
        device_id=device, device_id_type=MESH,
    )


def kernel(
    n_frames, n_pix,
    owner_ref, counts_hbm, flat_ref, diag_ref, off_ref,
    counts, own, frames_s, sum_rows, weights, stats, totals, rows, cols,
    prod, core_in, z_out, z_in, last_out, last_in,
    load_sem, data_send, data_recv, stat_send, stat_recv, tot_send, tot_recv,
    core_send, core_recv, z_send, z_recv, last_send, last_recv,
):
    square = n_frames == 4
    n_z = n_pix // CORES
    stages = n_z.bit_length() - 1
    block = lax.axis_index("frames")
    pix = lax.axis_index("pix")
    z, core = pix // CORES, lax.rem(pix, CORES)
    n_rows, n_slots = counts.shape
    half = n_slots // 2
    piece = n_rows // n_pix
    pair = CORES * piece
    x = lax.rem(block, 2)
    outer = jnp.logical_or(block == 0, block == 3)
    inner = jnp.logical_not(outer)
    across = block + 1 - 2 * x
    up = lax.rem(block + 2, 4)
    me = block if square else 0
    has_next, has_prev = block < n_frames - 1, block > 0
    follow = jnp.minimum(block + 1, n_frames - 1)
    before = jnp.maximum(block - 1, 0)

    def load(q):
        part = pl.ds(q * pair, pair)
        return pltpu.make_async_copy(counts_hbm.at[part], counts.at[part], load_sem.at[q])

    for q in range(n_z):
        load(q).start()

    barrier = pltpu.get_barrier_semaphore()
    for d in range(1, n_pix):
        pl.semaphore_signal(barrier, inc=1, device_id={"pix": lax.rem(pix + d, n_pix)}, device_id_type=MESH)
    if square:
        for d in range(1, 4):
            pl.semaphore_signal(barrier, inc=1, device_id={"frames": lax.rem(block + d, 4)}, device_id_type=MESH)
        pl.semaphore_wait(barrier, n_pix - 1 + 3)
    else:
        @pl.when(has_next)
        def _():
            pl.semaphore_signal(barrier, inc=1, device_id={"frames": follow}, device_id_type=MESH)

        @pl.when(has_prev)
        def _():
            pl.semaphore_signal(barrier, inc=1, device_id={"frames": before}, device_id_type=MESH)

        pl.semaphore_wait(barrier, n_pix - 1 + has_next.astype(jnp.int32) + has_prev.astype(jnp.int32))

    if square:
        always = block >= 0
        streams = ((0, 1 - x, across, always, always), (1, x, up, inner, outer))
    else:
        streams = ((0, 0, follow, has_next, has_prev), (1, 1, follow, has_next, has_prev))

    def data(slot, which, target, q):
        return remote(
            own.at[which, q], frames_s.at[2 + slot, q],
            data_send.at[slot, q], data_recv.at[slot, q], {"frames": target},
        )

    pixel_total = owner_ref[0]
    for i in range(1, n_pix):
        pixel_total = pixel_total + owner_ref[i]
    pixel_total = pixel_total.astype(F32)
    limit = owner_ref[pix]
    slot_ids = lax.broadcasted_iota(jnp.int32, (16, n_slots), 1)
    valid = (slot_ids < limit).astype(F32)
    weight = flat_ref[...] * valid
    weights[...] = weight
    first = weight.astype(BF16).astype(F32)
    second = (weight - first).astype(BF16).astype(F32)
    third = weight - first - second
    line = lax.broadcasted_iota(jnp.int32, (16, n_slots), 0)
    none = jnp.zeros_like(weight)
    split = jnp.where(line == 0, first, jnp.where(line == 1, second, jnp.where(line == 2, third, none)))
    filler = jnp.zeros((LANES - 16, n_slots), BF16)
    for i, value in enumerate((split, jnp.where(line == 3, weight * weight, none))):
        sum_rows[i, 0:16, :] = value.astype(BF16)
        sum_rows[i, 16:LANES, :] = filler

    stats[pix] = jnp.zeros((8, n_rows), F32)
    small = 16
    band = min(piece, 32)
    @pl.loop(0, n_z)
    def _(q):
        load(q).wait()

        @pl.loop(0, piece // small)
        def _(i):
            for c in range(CORES):
                for h in range(2):
                    taken = counts[pl.ds(q * pair + c * piece + i * small, small), h * half:(h + 1) * half]
                    own[h, q, c, pl.ds(i * small, small), :] = taken.astype(F32).astype(BF16)

        for slot, which, target, sends, _ in streams:
            @pl.when(sends)
            def _(slot=slot, which=which, target=target):
                data(slot, which, target, q).start()

    @pl.loop(0, n_z)
    def _(q):
        sums = jnp.zeros((pair, LANES), F32)
        for h in range(2):
            held = own[h, q].reshape(pair, half)
            lanes = slice(h * half, (h + 1) * half)
            sums = sums + dot_rows(held, sum_rows[0, :, lanes]) + dot_rows(held * held, sum_rows[1, :, lanes])
        sums = jnp.transpose(sums)
        part = pl.ds(pl.multiple_of(q * pair, LANES), pair)
        stats[pix, 0:1, part] = sums[0:1] + sums[1:2] + sums[2:3]
        stats[pix, 1:2, part] = sums[3:4]

    def stat(d):
        return remote(
            stats.at[pix], stats.at[pix], stat_send.at[d], stat_recv.at[pix],
            {"pix": lax.rem(pix + d, n_pix)},
        )

    def stat_from(d):
        source = lax.rem(pix + d, n_pix)
        return remote(stats.at[source], stats.at[source], stat_send.at[d], stat_recv.at[source], {"pix": source})

    for d in range(1, n_pix):
        stat(d).start()
    for d in range(1, n_pix):
        stat_from(d).wait_recv()
    total = stats[0]
    for i in range(1, n_pix):
        total = total + stats[i]
    totals[me] = total

    if square:
        def tot(d):
            return remote(totals.at[me], totals.at[me], tot_send.at[d], tot_recv.at[me], {"frames": lax.rem(block + d, 4)})

        def tot_from(d):
            source = lax.rem(block + d, 4)
            return remote(totals.at[source], totals.at[source], tot_send.at[d], tot_recv.at[source], {"frames": source})

        for d in range(1, 4):
            tot(d).start()
    else:
        def tot_next():
            return remote(totals.at[0], totals.at[1], tot_send.at[0], tot_recv.at[0], {"frames": follow})

        @pl.when(has_next)
        def _():
            tot_next().start()

    def take(index):
        held = totals[index]
        inverse_mean = pixel_total / held[0:1]
        norm = jnp.sqrt(held[1:2]) * inverse_mean
        scale = LEVELS ** 0.5 / norm
        rows[index, 0:1, :] = scale
        rows[index, 1:2, :] = 1.0 / scale
        for i, value in enumerate((inverse_mean, scale, 1.0 / scale)):
            column = jnp.transpose(jnp.broadcast_to(value, (LANES, n_rows)))
            cols[index, i] = column.reshape(n_z, CORES, piece, LANES)

    take(me)

    def scale_frames(src, src_index, dst_index, first_lane, q, index):
        @pl.loop(0, piece // small)
        def _(i):
            at = pl.ds(i * small, small)
            for c in range(CORES):
                inverse = cols[index, 0, q, c, at, :]
                for g in range(0, half, LANES):
                    weight = weights[0:1, pl.ds(pl.multiple_of(first_lane + g, LANES), LANES)]
                    frame = src[src_index, q, c, at, g:g + LANES].astype(F32) * weight
                    frames_s[dst_index, q, c, at, g:g + LANES] = (frame * inverse).astype(BF16)

    for h in range(2):
        @pl.loop(0, n_z)
        def _(q):
            scale_frames(own, h, h, h * half, q, me)

    other = 1 - core
    everything = slice(None)

    def lanes_of(n):
        return pl.ds(pl.multiple_of(n * pair, LANES), pair)

    def by_rows(body):
        @pl.loop(0, piece // band)
        def _(i):
            body(pl.ds(pl.multiple_of(i * band, band), band))

    def core_columns(k, n):
        return remote(
            prod.at[k, :, other, :, lanes_of(n)], core_in.at[k, :, :, lanes_of(n)],
            core_send.at[k, n], core_recv.at[k, n], {"pix": z * CORES + other},
        )

    def core_rows(k, j):
        return remote(
            prod.at[k, j, other], core_in.at[k, j],
            core_send.at[k, j], core_recv.at[k, j], {"pix": z * CORES + other},
        )

    def multiply_columns(k, pairs, n):
        out = None
        for left, right in pairs:
            term = dot_rows(frames_s[left].reshape(n_rows, half), frames_s[right, n].reshape(pair, half))
            out = term if out is None else out + term
        prod[k, :, :, :, lanes_of(n)] = out.reshape(n_z, CORES, piece, pair)
        core_columns(k, n).start()

    def merge_columns(k, n, row_block, col_block):
        core_columns(k, n).wait()

        @pl.loop(0, n_z)
        def _(j):
            def body(at):
                value = prod[k, j, core, at, lanes_of(n)] + core_in[k, j, at, lanes_of(n)]
                value = value * widened(cols[row_block, 1, j, core, at, :], pair)
                prod[k, j, core, at, lanes_of(n)] = value * rows[col_block, 0:1, lanes_of(n)]

            by_rows(body)

    def multiply_rows(k, left, right, j):
        @pl.loop(0, n_z)
        def _(n):
            out = dot_rows(frames_s[left, j].reshape(pair, half), frames_s[right, n].reshape(pair, half))
            prod[k, j, :, :, lanes_of(n)] = out.reshape(CORES, piece, pair)

        core_rows(k, j).start()

    def merge_rows(k, j, row_block, col_block):
        core_rows(k, j).wait()

        def body(at):
            value = (prod[k, j, core, at, :] + core_in[k, j, at, :]) * widened(cols[row_block, 1, j, core, at, :], n_rows)
            prod[k, j, core, at, :] = value * rows[col_block, 0:1, :]

        by_rows(body)

    def product(k, pairs, row_block, col_block):
        @pl.loop(0, n_z)
        def _(n):
            multiply_columns(k, pairs, n)

        @pl.loop(0, n_z)
        def _(n):
            merge_columns(k, n, row_block, col_block)

    def z_copy(k, s, m, part, c):
        bit = 1 << s
        sign = 1 - 2 * lax.rem(z // bit, 2)
        at = n_z - (n_z >> s) + m
        return remote(
            z_out.at[k, at, :, part], z_in.at[k, at, :, part], z_send.at[k, at, c], z_recv.at[k, at, c],
            {"pix": (z + sign * bit) * CORES + core},
        )

    def z_put(k, s, m, part=everything, c=0):
        bit = 1 << s
        j = m * 2 * bit + (1 - lax.rem(z // bit, 2)) * bit + lax.rem(z, bit)

        def body(at):
            z_out[k, n_z - (n_z >> s) + m, at, part] = quantized(prod[k, j, core, at, part])

        by_rows(body)
        z_copy(k, s, m, part, c).start()

    def z_get(k, s, m, part=everything, c=0, both=True):
        bit = 1 << s
        copy = z_copy(k, s, m, part, c)
        copy.wait_recv()
        if both:
            copy.wait_send()
        j = m * 2 * bit + lax.rem(z, 2 * bit)

        def body(at):
            came = restored(z_in[k, n_z - (n_z >> s) + m, at, part])
            prod[k, j, core, at, part] = prod[k, j, core, at, part] + came

        by_rows(body)

    def order(s):
        count = n_z >> (s + 1)
        if count == 1:
            return [0], []
        held = lax.rem(z // (2 << s), 2)
        return [2 * i + 1 - held for i in range(count // 2)], [2 * i + held for i in range(count // 2)]

    def advance(k, s, part=everything, c=0):
        ahead, after = order(s) if s >= 0 else ((), ())
        for m in ahead:
            z_get(k, s, m, part, c)
        if s + 1 < stages:
            for m in sum(order(s + 1), []):
                z_put(k, s + 1, m, part, c)
        for m in after:
            z_get(k, s, m, part, c)

    def at_stage(s, j, sends):
        bit, j = 1 << s, jnp.int32(j)
        same = lax.rem(z // bit, 2) == lax.rem(j // bit, 2)
        return jnp.logical_and(lax.rem(z, bit) == lax.rem(j, bit), jnp.logical_not(same) if sends else same)

    def advance_rows(k, s, j):
        if s >= 0:
            @pl.when(at_stage(s, j, False))
            def _():
                z_get(k, s, j // (2 << s), both=False)
        if s + 1 < stages:
            @pl.when(at_stage(s + 1, j, True))
            def _():
                z_put(k, s + 1, j // (2 << (s + 1)))

    def finish_diag():
        advance(0, stages - 1)

        def body(at):
            value = prod[0, z, core, at, :] * widened(cols[me, 2, z, core, at, :], n_rows)
            diag_ref[at, :] = value * (rows[me, 1:2, :] * inverse_total)

        by_rows(body)

    def receive(q):
        for slot, which, target, _, arrives in streams:
            @pl.when(arrives)
            def _(slot=slot, which=which, target=target):
                data(slot, which, target, q).wait_recv()
                source = (across if slot == 0 else up) if square else 1
                scale_frames(frames_s, 2 + slot, 2 + slot, (x if square else slot) * half, q, source)

    inverse_total = 1.0 / jnp.full((1, 1), pixel_total, F32)
    product(0, ((0, 0), (1, 1)), me, me)
    advance(0, -1)

    if square:
        for d in range(1, 4):
            tot_from(d).wait_recv()

        @pl.loop(1, 4)
        def _(d):
            take(lax.rem(block + d, 4))
    else:
        @pl.when(has_prev)
        def _():
            tot_next().wait_recv()
            take(1)

    if square:
        even = x == 0
        odd = x == 1

        def last(source, slot, target):
            return remote(last_out.at[source], last_in.at[slot], last_send.at[source], last_recv.at[slot], {"frames": target})

        def pack(slot, k):
            def body(at):
                last_out[slot, at, :] = quantized(prod[k, z, core, at, :])

            by_rows(body)

        def onward(q, s):
            @pl.when(even)
            def _():
                advance_rows(1, s, q)

            @pl.when(odd)
            def _():
                advance(1, s, lanes_of(q), q)

        @pl.loop(0, n_z)
        def _(q):
            receive(q)

            @pl.when(even)
            def _():
                multiply_rows(1, 2, 0, q)
                merge_rows(1, q, across, block)

            @pl.when(odd)
            def _():
                multiply_columns(1, ((1, 2),), q)
                merge_columns(1, q, block, across)

            onward(q, -1)
            for s in range(stages):
                @pl.when(q > s)
                def _(s=s):
                    onward(q - 1 - s, s)

            @pl.when(q == 0)
            def _():
                for s in range(stages - 1):
                    advance(0, s)

        @pl.when(outer)
        def _():
            product(2, ((jnp.where(even, 3, 2), jnp.where(even, 2, 3)),), 2, 1)
            advance(2, -1)

        remaining = [(q, s) for q in range(n_z) for s in range(max(n_z - 1 - q, 0), stages)]
        for q, s in remaining[:-1]:
            onward(q, s)

        @pl.when(outer)
        def _():
            for s in range(stages - 1):
                advance(2, s)

        for q, s in remaining[-1:]:
            onward(q, s)

        @pl.when(even)
        def _():
            pack(0, 1)
            last(0, 0, across).start()

        finish_diag()

        @pl.when(outer)
        def _():
            advance(2, stages - 1)
            pack(1, 2)

        @pl.when(block == 0)
        def _():
            last(1, 1, up).start()

        @pl.when(block == 3)
        def _():
            last(1, 0, across).start()

        def write(value):
            def body(at):
                scale = widened(cols[block, 2, z, core, at, :], n_rows)
                off_ref[at, :] = value(at) * scale * (rows[before, 1:2, :] * inverse_total)

            by_rows(body)

        @pl.when(block == 0)
        def _():
            off_ref[...] = jnp.zeros_like(off_ref)

        @pl.when(odd)
        def _():
            last(0, 0, across).wait_recv()
            write(lambda at: prod[1, z, core, at, :] + restored(last_in[0, at, :]))

        @pl.when(block == 2)
        def _():
            last(0, 0, across).wait_recv()
            last(1, 1, up).wait_recv()
            write(lambda at: restored(last_in[0, at, :]) + restored(last_in[1, at, :]))

        @pl.when(even)
        def _():
            last(0, 0, across).wait_send()

            @pl.loop(0, n_z)
            def _(j):
                for s in range(stages):
                    @pl.when(at_stage(s, j, True))
                    def _(s=s):
                        z_copy(1, s, j // (2 << s), everything, 0).wait_send()

        @pl.when(outer)
        def _():
            last(1, 1, up).wait_send()
    else:
        for s in range(stages - 1):
            advance(0, s)
        for q in range(n_z):
            receive(q)

        @pl.when(has_prev)
        def _():
            product(1, ((0, 2), (1, 3)), 0, 1)
            for s in range(-1, stages):
                advance(1, s)
            off_ref[...] = prod[1, z, core] * widened(cols[0, 2, z, core], n_rows) * (rows[1, 1:2, :] * inverse_total)

        @pl.when(jnp.logical_not(has_prev))
        def _():
            off_ref[...] = jnp.zeros_like(off_ref)

        finish_diag()

    for d in range(1, n_pix):
        stat(d).wait_send()
    if square:
        for d in range(1, 4):
            tot(d).wait_send()
    else:
        @pl.when(has_next)
        def _():
            tot_next().wait_send()
    for q in range(n_z):
        for slot, which, target, sends, _ in streams:
            @pl.when(sends)
            def _(slot=slot, which=which, target=target):
                data(slot, which, target, q).wait_send()


def on_device(n_frames, n_pix, photon_counts, flat_field, owner_counts):
    n_rows, n_slots = photon_counts.shape
    half, piece, n_z = n_slots // 2, n_rows // n_pix, n_pix // CORES
    tiles, blocks = (3, 4) if n_frames == 4 else (2, 2)
    sent = max(n_z - 1, 1)
    flat = flat_field[None, :]
    out = jax.ShapeDtypeStruct((piece, n_rows), F32)
    dma = pltpu.SemaphoreType.DMA
    return pl.pallas_call(
        functools.partial(kernel, n_frames, n_pix),
        out_shape=(out, out),
        in_specs=[
            pl.BlockSpec(memory_space=pltpu.SMEM),
            pl.BlockSpec(memory_space=pl.ANY),
            pl.BlockSpec(memory_space=pltpu.VMEM),
        ],
        out_specs=(pl.BlockSpec(memory_space=pltpu.VMEM),) * 2,
        scratch_shapes=[
            pltpu.VMEM((n_rows, n_slots), jnp.int32),
            pltpu.VMEM((2, n_z, CORES, piece, half), BF16),
            pltpu.VMEM((4, n_z, CORES, piece, half), BF16),
            pltpu.VMEM((2, LANES, n_slots), BF16),
            pltpu.VMEM((16, n_slots), F32),
            pltpu.VMEM((n_pix, 8, n_rows), F32),
            pltpu.VMEM((blocks, 8, n_rows), F32),
            pltpu.VMEM((blocks, 8, n_rows), F32),
            pltpu.VMEM((blocks, 3, n_z, CORES, piece, LANES), F32),
            pltpu.VMEM((tiles, n_z, CORES, piece, n_rows), F32),
            pltpu.VMEM((tiles, n_z, piece, n_rows), F32),
            pltpu.VMEM((tiles, sent, piece, n_rows), jnp.int16),
            pltpu.VMEM((tiles, sent, piece, n_rows), jnp.int16),
            pltpu.VMEM((2, piece, n_rows), jnp.int16),
            pltpu.VMEM((2, piece, n_rows), jnp.int16),
            dma((n_z,)),
            dma((2, n_z)), dma((2, n_z)),
            dma((n_pix,)), dma((n_pix,)),
            dma((4,)), dma((4,)),
            dma((tiles, n_z)), dma((tiles, n_z)),
            dma((tiles, sent, n_z)), dma((tiles, sent, n_z)),
            dma((2,)), dma((2,)),
        ],
        compiler_params=pltpu.CompilerParams(
            collective_id=0, has_side_effects=True, vmem_limit_bytes=62 * 1024 * 1024
        ),
        cost_estimate=pl.CostEstimate(
            flops=4 * n_rows * n_rows * n_slots, bytes_accessed=4 * n_rows * n_slots, transcendentals=0
        ),
    )(owner_counts, photon_counts, flat)


def solution(mesh):
    return jax.shard_map(
        functools.partial(on_device, mesh.shape["frames"], mesh.shape["pix"]),
        mesh=mesh,
        in_specs=(P("frames", "pix"), P("pix"), P()),
        out_specs=(P(("frames", "pix"), None), P(("frames", "pix"), None)),
        check_vma=False,
    )
```

```python
import functools

import jax
import jax.numpy as jnp
from jax import lax
from jax.experimental import pallas as pl
from jax.experimental.pallas import tpu as pltpu
from jax.sharding import PartitionSpec as P

MESH = pl.DeviceIdType.MESH
F32, BF16 = jnp.float32, jnp.bfloat16
LANES = 128
LEVELS = 64000.0
OFFSET = 32768
CORES = 2


def dot_rows(left, right):
    return lax.dot_general(left, right, (((1,), (1,)), ((), ())), preferred_element_type=F32)


def widened(column, lanes):
    count = lanes // LANES
    return column if count == 1 else jnp.concatenate([column] * count, axis=-1)


def quantized(value):
    return ((value + 0.5).astype(jnp.int32) - OFFSET).astype(jnp.int16)


def restored(value):
    return (value.astype(jnp.int32) + OFFSET).astype(F32)


def remote(src, dst, send_sem, recv_sem, device):
    return pltpu.make_async_remote_copy(
        src_ref=src, dst_ref=dst, send_sem=send_sem, recv_sem=recv_sem,
        device_id=device, device_id_type=MESH,
    )


def kernel(
    n_frames, n_pix,
    owner_ref, counts_hbm, flat_ref, diag_ref, off_ref,
    counts, own, frames_s, sum_rows, weights, stats, totals, rows, cols,
    core_out, core_in, acc, z_out, z_in, last_out, last_in,
    load_sem, data_send, data_recv, stat_send, stat_recv, tot_send, tot_recv,
    core_send, core_recv, z_send, z_recv, last_send, last_recv,
):
    square = n_frames == 4
    n_z = n_pix // CORES
    stages = n_z.bit_length() - 1
    block = lax.axis_index("frames")
    pix = lax.axis_index("pix")
    z, core = pix // CORES, lax.rem(pix, CORES)
    n_rows, n_slots = counts.shape
    half = n_slots // 2
    piece = n_rows // n_pix
    pair = CORES * piece
    x = lax.rem(block, 2)
    outer = jnp.logical_or(block == 0, block == 3)
    inner = jnp.logical_not(outer)
    across = block + 1 - 2 * x
    up = lax.rem(block + 2, 4)
    me = block if square else 0
    has_next, has_prev = block < n_frames - 1, block > 0
    follow = jnp.minimum(block + 1, n_frames - 1)
    before = jnp.maximum(block - 1, 0)

    def load(q):
        part = pl.ds(q * pair, pair)
        return pltpu.make_async_copy(counts_hbm.at[part], counts.at[part], load_sem.at[q])

    for q in range(n_z):
        load(q).start()

    barrier = pltpu.get_barrier_semaphore()
    for d in range(1, n_pix):
        pl.semaphore_signal(barrier, inc=1, device_id={"pix": lax.rem(pix + d, n_pix)}, device_id_type=MESH)
    if square:
        for d in range(1, 4):
            pl.semaphore_signal(barrier, inc=1, device_id={"frames": lax.rem(block + d, 4)}, device_id_type=MESH)
        pl.semaphore_wait(barrier, n_pix - 1 + 3)
    else:
        @pl.when(has_next)
        def _():
            pl.semaphore_signal(barrier, inc=1, device_id={"frames": follow}, device_id_type=MESH)

        @pl.when(has_prev)
        def _():
            pl.semaphore_signal(barrier, inc=1, device_id={"frames": before}, device_id_type=MESH)

        pl.semaphore_wait(barrier, n_pix - 1 + has_next.astype(jnp.int32) + has_prev.astype(jnp.int32))

    if square:
        always = block >= 0
        streams = ((0, 1 - x, across, always, always), (1, x, up, inner, outer))
    else:
        streams = ((0, 0, follow, has_next, has_prev), (1, 1, follow, has_next, has_prev))

    def data(slot, which, target, q):
        return remote(
            own.at[which, q], frames_s.at[2 + slot, q],
            data_send.at[slot, q], data_recv.at[slot, q], {"frames": target},
        )

    pixel_total = owner_ref[0]
    for i in range(1, n_pix):
        pixel_total = pixel_total + owner_ref[i]
    pixel_total = pixel_total.astype(F32)
    limit = owner_ref[pix]
    slot_ids = lax.broadcasted_iota(jnp.int32, (16, n_slots), 1)
    valid = (slot_ids < limit).astype(F32)
    weight = flat_ref[...] * valid
    weights[...] = weight
    first = weight.astype(BF16).astype(F32)
    second = (weight - first).astype(BF16).astype(F32)
    third = weight - first - second
    line = lax.broadcasted_iota(jnp.int32, (16, n_slots), 0)
    none = jnp.zeros_like(weight)
    split = jnp.where(line == 0, first, jnp.where(line == 1, second, jnp.where(line == 2, third, none)))
    filler = jnp.zeros((LANES - 16, n_slots), BF16)
    for i, value in enumerate((split, jnp.where(line == 3, weight * weight, none))):
        sum_rows[i, 0:16, :] = value.astype(BF16)
        sum_rows[i, 16:LANES, :] = filler

    stats[pix] = jnp.zeros((8, n_rows), F32)
    small = 16
    for q in range(n_z):
        load(q).wait()

        @pl.loop(0, piece // small)
        def _(i):
            for c in range(CORES):
                for h in range(2):
                    taken = counts[pl.ds(q * pair + c * piece + i * small, small), h * half:(h + 1) * half]
                    own[h, q, c, pl.ds(i * small, small), :] = taken.astype(F32).astype(BF16)

        for slot, which, target, sends, _ in streams:
            @pl.when(sends)
            def _(slot=slot, which=which, target=target):
                data(slot, which, target, q).start()

    for q in range(n_z):
        sums = jnp.zeros((pair, LANES), F32)
        for h in range(2):
            held = own[h, q].reshape(pair, half)
            lanes = slice(h * half, (h + 1) * half)
            sums = sums + dot_rows(held, sum_rows[0, :, lanes]) + dot_rows(held * held, sum_rows[1, :, lanes])
        sums = jnp.transpose(sums)
        part = slice(q * pair, (q + 1) * pair)
        stats[pix, 0:1, part] = sums[0:1] + sums[1:2] + sums[2:3]
        stats[pix, 1:2, part] = sums[3:4]

    def stat(d):
        return remote(
            stats.at[pix], stats.at[pix], stat_send.at[d], stat_recv.at[pix],
            {"pix": lax.rem(pix + d, n_pix)},
        )

    def stat_from(d):
        source = lax.rem(pix + d, n_pix)
        return remote(stats.at[source], stats.at[source], stat_send.at[d], stat_recv.at[source], {"pix": source})

    for d in range(1, n_pix):
        stat(d).start()
    for d in range(1, n_pix):
        stat_from(d).wait_recv()
    total = stats[0]
    for i in range(1, n_pix):
        total = total + stats[i]
    totals[me] = total

    if square:
        def tot(d):
            return remote(totals.at[me], totals.at[me], tot_send.at[d], tot_recv.at[me], {"frames": lax.rem(block + d, 4)})

        def tot_from(d):
            source = lax.rem(block + d, 4)
            return remote(totals.at[source], totals.at[source], tot_send.at[d], tot_recv.at[source], {"frames": source})

        for d in range(1, 4):
            tot(d).start()
    else:
        def tot_next():
            return remote(totals.at[0], totals.at[1], tot_send.at[0], tot_recv.at[0], {"frames": follow})

        @pl.when(has_next)
        def _():
            tot_next().start()

    def take(index):
        held = totals[index]
        inverse_mean = pixel_total / held[0:1]
        norm = jnp.sqrt(held[1:2]) * inverse_mean
        scale = LEVELS ** 0.5 / norm
        rows[index, 0:1, :] = scale
        rows[index, 1:2, :] = 1.0 / scale
        for i, value in enumerate((inverse_mean, scale, 1.0 / scale)):
            column = jnp.transpose(jnp.broadcast_to(value, (LANES, n_rows)))
            cols[index, i] = column.reshape(n_z, CORES, piece, LANES)

    take(me)

    def scale_frames(src, src_index, dst_index, first_lane, q, index):
        @pl.loop(0, piece // small)
        def _(i):
            at = pl.ds(i * small, small)
            for c in range(CORES):
                inverse = cols[index, 0, q, c, at, :]
                for g in range(0, half, LANES):
                    weight = weights[0:1, pl.ds(pl.multiple_of(first_lane + g, LANES), LANES)]
                    frame = src[src_index, q, c, at, g:g + LANES].astype(F32) * weight
                    frames_s[dst_index, q, c, at, g:g + LANES] = (frame * inverse).astype(BF16)

    for h in range(2):
        @pl.loop(0, n_z)
        def _(q):
            scale_frames(own, h, h, h * half, q, me)

    def product(k, pairs, row_block, col_block):
        other = 1 - core

        def at(n):
            return pl.ds(pl.multiple_of(n * pair, LANES), pair)

        def core_copy(n):
            return remote(
                core_out.at[k, :, :, at(n)], core_in.at[k, :, :, at(n)],
                core_send.at[k, n], core_recv.at[k, n], {"pix": z * CORES + other},
            )

        def tile(side, n):
            out = None
            for left, right in pairs:
                term = dot_rows(
                    frames_s[left, :, side].reshape(n_z * piece, half),
                    frames_s[right, n].reshape(pair, half),
                )
                out = term if out is None else out + term
            out = out.reshape(n_z, piece, pair) * widened(cols[row_block, 1, :, side], pair)
            return out * rows[col_block, 0:1, at(n)]

        @pl.loop(0, n_z)
        def _(n):
            core_out[k, :, :, at(n)] = quantized(tile(other, n))
            core_copy(n).start()

        @pl.loop(0, n_z)
        def _(n):
            value = tile(core, n)
            core_copy(n).wait()
            acc[k, :, :, at(n)] = value + restored(core_in[k, :, :, at(n)])

    def z_base(s):
        return n_z - (n_z >> s)

    def z_copy(k, s, m):
        bit = 1 << s
        sign = 1 - 2 * lax.rem(z // bit, 2)
        at = z_base(s) + m
        return remote(
            z_out.at[k, at], z_in.at[k, at], z_send.at[k, at], z_recv.at[k, at],
            {"pix": (z + sign * bit) * CORES + core},
        )

    def z_send_stage(k, s):
        bit = 1 << s
        low, top = lax.rem(z, bit), lax.rem(z // bit, 2)
        for m in range(n_z >> (s + 1)):
            j = m * 2 * bit + (1 - top) * bit + low
            z_out[k, z_base(s) + m] = quantized(acc[k, j])
            z_copy(k, s, m).start()

    def z_recv_stage(k, s):
        bit = 1 << s
        for m in range(n_z >> (s + 1)):
            z_copy(k, s, m).wait()
            j = m * 2 * bit + lax.rem(z, 2 * bit)
            acc[k, j] = acc[k, j] + restored(z_in[k, z_base(s) + m])

    def diag_steps(first_stage, end_stage):
        for s in range(max(first_stage, 0), end_stage):
            z_recv_stage(0, s)
            if s + 1 < stages:
                z_send_stage(0, s + 1)

    def finish_diag():
        diag_steps(stages - 1, stages)
        diag_ref[...] = acc[0, z] * widened(cols[me, 2, z, core], n_rows) * (rows[me, 1:2, :] * inverse_total)

    def receive(q):
        for slot, which, target, _, arrives in streams:
            @pl.when(arrives)
            def _(slot=slot, which=which, target=target):
                data(slot, which, target, q).wait_recv()
                source = (across if slot == 0 else up) if square else 1
                scale_frames(frames_s, 2 + slot, 2 + slot, (x if square else slot) * half, q, source)

    inverse_total = 1.0 / jnp.full((1, 1), pixel_total, F32)
    product(0, ((0, 0), (1, 1)), me, me)
    if stages:
        z_send_stage(0, 0)

    if square:
        for d in range(1, 4):
            tot_from(d).wait_recv()
        for d in range(1, 4):
            take(lax.rem(block + d, 4))
    else:
        @pl.when(has_prev)
        def _():
            tot_next().wait_recv()
            take(1)

    for q in range(n_z - 1):
        receive(q)
    diag_steps(0, stages - 1)
    receive(n_z - 1)

    if square:
        even = x == 0
        later, sooner = jnp.maximum(block, across), jnp.minimum(block, across)

        def last(source, slot, target):
            return remote(last_out.at[source], last_in.at[slot], last_send.at[source], last_recv.at[slot], {"frames": target})

        def send_last(k):
            if k == 1:
                @pl.when(even)
                def _():
                    last_out[0] = quantized(acc[1, z])
                    last(0, 0, across).start()
            else:
                last_out[1] = quantized(acc[2, z])

                @pl.when(block == 0)
                def _():
                    last(1, 1, up).start()

                @pl.when(block == 3)
                def _():
                    last(1, 0, across).start()

        def advance(k, s):
            if s >= 0:
                z_recv_stage(k, s)
            if s + 1 < stages:
                z_send_stage(k, s + 1)
            else:
                send_last(k)

        product(1, ((jnp.where(even, 2, 1), jnp.where(even, 0, 2)),), later, sooner)
        advance(1, -1)

        @pl.when(outer)
        def _():
            product(2, ((jnp.where(even, 3, 2), jnp.where(even, 2, 3)),), 2, 1)
            advance(2, -1)

        finish_diag()
        for s in range(stages):
            advance(1, s)

            @pl.when(outer)
            def _(s=s):
                advance(2, s)

        def write(value):
            off_ref[...] = value * widened(cols[block, 2, z, core], n_rows) * (rows[before, 1:2, :] * inverse_total)

        @pl.when(block == 0)
        def _():
            off_ref[...] = jnp.zeros_like(off_ref)

        @pl.when(x == 1)
        def _():
            last(0, 0, across).wait_recv()
            write(acc[1, z] + restored(last_in[0]))

        @pl.when(block == 2)
        def _():
            last(0, 0, across).wait_recv()
            last(1, 1, up).wait_recv()
            write(restored(last_in[0]) + restored(last_in[1]))

        @pl.when(even)
        def _():
            last(0, 0, across).wait_send()

        @pl.when(outer)
        def _():
            last(1, 1, up).wait_send()
    else:
        @pl.when(has_prev)
        def _():
            product(1, ((0, 2), (1, 3)), 0, 1)
            for s in range(stages):
                z_send_stage(1, s)
                z_recv_stage(1, s)
            off_ref[...] = acc[1, z] * widened(cols[0, 2, z, core], n_rows) * (rows[1, 1:2, :] * inverse_total)

        @pl.when(jnp.logical_not(has_prev))
        def _():
            off_ref[...] = jnp.zeros_like(off_ref)

        finish_diag()

    for d in range(1, n_pix):
        stat(d).wait_send()
    if square:
        for d in range(1, 4):
            tot(d).wait_send()
    else:
        @pl.when(has_next)
        def _():
            tot_next().wait_send()
    for q in range(n_z):
        for slot, which, target, sends, _ in streams:
            @pl.when(sends)
            def _(slot=slot, which=which, target=target):
                data(slot, which, target, q).wait_send()


def on_device(n_frames, n_pix, photon_counts, flat_field, owner_counts):
    n_rows, n_slots = photon_counts.shape
    half, piece, n_z = n_slots // 2, n_rows // n_pix, n_pix // CORES
    tiles, blocks = (3, 4) if n_frames == 4 else (2, 2)
    sent = max(n_z - 1, 1)
    flat = flat_field[None, :]
    out = jax.ShapeDtypeStruct((piece, n_rows), F32)
    dma = pltpu.SemaphoreType.DMA
    return pl.pallas_call(
        functools.partial(kernel, n_frames, n_pix),
        out_shape=(out, out),
        in_specs=[
            pl.BlockSpec(memory_space=pltpu.SMEM),
            pl.BlockSpec(memory_space=pl.ANY),
            pl.BlockSpec(memory_space=pltpu.VMEM),
        ],
        out_specs=(pl.BlockSpec(memory_space=pltpu.VMEM),) * 2,
        scratch_shapes=[
            pltpu.VMEM((n_rows, n_slots), jnp.int32),
            pltpu.VMEM((2, n_z, CORES, piece, half), BF16),
            pltpu.VMEM((4, n_z, CORES, piece, half), BF16),
            pltpu.VMEM((2, LANES, n_slots), BF16),
            pltpu.VMEM((16, n_slots), F32),
            pltpu.VMEM((n_pix, 8, n_rows), F32),
            pltpu.VMEM((blocks, 8, n_rows), F32),
            pltpu.VMEM((blocks, 8, n_rows), F32),
            pltpu.VMEM((blocks, 3, n_z, CORES, piece, LANES), F32),
            pltpu.VMEM((tiles, n_z, piece, n_rows), jnp.int16),
            pltpu.VMEM((tiles, n_z, piece, n_rows), jnp.int16),
            pltpu.VMEM((tiles, n_z, piece, n_rows), F32),
            pltpu.VMEM((tiles, sent, piece, n_rows), jnp.int16),
            pltpu.VMEM((tiles, sent, piece, n_rows), jnp.int16),
            pltpu.VMEM((2, piece, n_rows), jnp.int16),
            pltpu.VMEM((2, piece, n_rows), jnp.int16),
            dma((n_z,)),
            dma((2, n_z)), dma((2, n_z)),
            dma((n_pix,)), dma((n_pix,)),
            dma((4,)), dma((4,)),
            dma((tiles, n_z)), dma((tiles, n_z)),
            dma((tiles, sent)), dma((tiles, sent)),
            dma((2,)), dma((2,)),
        ],
        compiler_params=pltpu.CompilerParams(
            collective_id=0, has_side_effects=True, vmem_limit_bytes=62 * 1024 * 1024
        ),
        cost_estimate=pl.CostEstimate(
            flops=4 * n_rows * n_rows * n_slots, bytes_accessed=4 * n_rows * n_slots, transcendentals=0
        ),
    )(owner_counts, photon_counts, flat)


def solution(mesh):
    return jax.shard_map(
        functools.partial(on_device, mesh.shape["frames"], mesh.shape["pix"]),
        mesh=mesh,
        in_specs=(P("frames", "pix"), P("pix"), P()),
        out_specs=(P(("frames", "pix"), None), P(("frames", "pix"), None)),
        check_vma=False,
    )
```
